256 devices in a mesh: gx: 8 (over y, x_lo), gy: 32 (over z, x_hi, core).
Axes of the slice: x: 4 (x_hi: 2, x_lo: 2; x = x_hi * 2 + x_lo), y: 4, z: 8, core: 2. Of those that a mesh axis runs over, the one named last changes fastest.
Arguments:
- features: bfloat16 [8, 32, 256, 256], P('gx', 'gy'), may hold values from -6 to 6
- displacement: float32 [8, 32, 3, 2048], P('gx', 'gy'), may hold values from -0.5 to 0.5, as said below
- neighbours: int32 [8, 32, 2048], P('gx', 'gy'), may hold values from 0 to 1791, as said below
- neighbour_count: int32 [8, 32, 256], P('gx', 'gy'), may hold values from 4 to 8, as said below
- species: int32 [8, 32, 256], P('gx', 'gy'), may hold values from 0 to 3
- send_list: int32 [8, 32, 8, 192], P('gx', 'gy'), may hold values from 0 to 255, as said below
- send_count: int32 [8, 32, 8], P('gx', 'gy'), may hold values from 96 to 192, as said below
- w_center: bfloat16 [256, 1024], replicated, may hold values from -0.375 to 0.375
- w_neighbour: bfloat16 [256, 1024], replicated, may hold values from -0.375 to 0.375
- w_radial: bfloat16 [8, 1024], replicated, may hold values from -4 to 4
- w_hidden: bfloat16 [1024, 1024], replicated, may hold values from -0.1875 to 0.1875
- w_tensor: bfloat16 [1024, 64], replicated, may hold values from -0.1875 to 0.1875
- readout: float32 [64], replicated, may hold values from -0.375 to 0.375
- species_scale: float32 [4], replicated, may hold values from 0.5 to 2
- species_shift: float32 [4], replicated, may hold values from -4 to 4
Outputs:
- atom_energy: float32 [8, 32, 256], P('gx', 'gy')
- forces: float32 [8, 32, 3, 256], P('gx', 'gy')
The draws below stay inside these ranges and needn't reach their ends.
Inputs may be any that keep to these rules, and one draw needn't show every extreme that they name: `send_count`: directions as in the reference program. For each direction some domain sends exactly 192 rows. `send_list`: each list holds distinct atoms in rising order. `neighbours`: rows 0..255 are own atoms, row 256 + b * 192 + k is row k of ghost block b; a ghost row always lies below the count of the list it came from. `neighbour_count`: some atom has all 8 slots live. `displacement`: each component's magnitude lies in 0.2 to 0.5.
All inputs are finite; a program needn't handle non-finite values.
Results may differ from the reference program's by a relative error of at most 0.018.
Values may be sent and summed in bfloat16 or wider, within the bound.
A program may use at most 128 MiB of HBM per device.

```python
import math
import jax
import jax.numpy as jnp
from jax import lax

A_DEV = 256
KMAX = 8
GMAX = 192
CH = 64
HID = 1024
NB = 8
NSPEC = 4
H = 256
EDGES = 2048
DOMX = 8
DOMY = 32


DIRECTIONS = ((-1, -1), (-1, 0), (-1, 1), (0, -1), (0, 1), (1, -1), (1, 0), (1, 1))


def count_table(key):
    domains = DOMX * DOMY
    counts = jax.random.randint(key, (domains, 8), GMAX // 2, GMAX + 1)
    chosen = jax.random.randint(jax.random.fold_in(key, 11), (8,), 0, domains)
    hitting = jnp.arange(domains)[:, None] == chosen[None, :]
    return jnp.where(hitting, GMAX, counts).astype(jnp.int32).reshape(DOMX, DOMY, 8)


def draw_send_count(key, part):
    return count_table(key)


def draw_send_list(key, part):
    key = jax.random.fold_in(key, 9)
    list_keys = jax.random.split(key, DOMX * DOMY * 8)
    lists = jax.vmap(lambda one_key: jnp.sort(jax.random.permutation(one_key, A_DEV)[:GMAX]))(list_keys)
    lists = lists.reshape(DOMX, DOMY, 8, GMAX)
    lists = lists.at[0, 0, 0].set(jnp.arange(GMAX) + (A_DEV - GMAX))
    lists = lists.at[0, 0, 7].set(jnp.arange(GMAX))
    return lists.astype(jnp.int32)


def draw_neighbours(key, part):
    counts = count_table(key)
    key = jax.random.fold_in(key, 5)
    first_key, second_key = jax.random.split(key)
    received = jnp.stack([jnp.roll(counts[:, :, 7 - direction], (-offset[0], -offset[1]), (0, 1)) for direction, offset in enumerate(DIRECTIONS)], axis=2)
    source = jax.random.randint(first_key, (DOMX, DOMY, EDGES), 0, 24)
    raw_slot = jax.random.randint(second_key, (DOMX, DOMY, EDGES), 0, 1 << 20)
    block_id = jnp.clip(source - 16, 0, 7)
    block_count = jnp.take_along_axis(received, block_id, axis=2)
    ghost_index = A_DEV + block_id * GMAX + raw_slot % block_count
    local_index = raw_slot % A_DEV
    return jnp.where(source < 16, local_index, ghost_index).astype(jnp.int32)


def draw_neighbour_count(key, part):
    key = jax.random.fold_in(key, 3)
    first_key, second_key = jax.random.split(key)
    total = DOMX * DOMY * A_DEV
    counts = jax.random.randint(first_key, (total,), KMAX // 2, KMAX + 1)
    chosen = jax.random.randint(second_key, (), 0, total)
    counts = jnp.where(jnp.arange(total) == chosen, KMAX, counts)
    return counts.astype(jnp.int32).reshape(DOMX, DOMY, A_DEV)


def draw_displacement(key, part):
    key = jax.random.fold_in(key, 7)
    first_key, second_key = jax.random.split(key)
    magnitude = jax.random.uniform(first_key, (DOMX, DOMY, 3, EDGES), jnp.float32, 0.2, 0.5)
    signs = jax.random.randint(second_key, (DOMX, DOMY, 3, EDGES), 0, 2) * 2 - 1
    return magnitude * signs.astype(jnp.float32)


def set_ends(values, own_key, smallest, high):
    spot = [jax.random.randint(jax.random.fold_in(own_key, axis), (), 0, length) for axis, length in enumerate(values.shape)]
    main_axis = values.shape.index(max(values.shape))
    neighbour = spot[:main_axis] + [(spot[main_axis] + 1) % values.shape[main_axis]] + spot[main_axis + 1:]
    return values.at[tuple(spot)].set(smallest).at[tuple(neighbour)].set(high)


def block_scale(own_key, dims, cuts, low, high):
    level, own = 1.0, jax.random.fold_in(own_key, 6)
    for position, shards_of in cuts:
        steps = jnp.exp(jax.random.uniform(jax.random.fold_in(own, position), (shards_of,), jnp.float32, low / len(cuts), high / len(cuts)))
        level = level * jnp.repeat(steps, dims[position] // shards_of).reshape([-1 if axis == position else 1 for axis in range(len(dims))])
    return level


def centred(rng, dims, spread, reach, cuts=(), dtype=jnp.bfloat16):
    entries = spread * jax.random.normal(rng, dims, jnp.float32)
    if cuts:
        entries = entries * block_scale(rng, dims, cuts, -0.22, 0.18)
    return jnp.clip(entries, -reach, reach).astype(dtype)


def setup_inputs(seed: int = 0) -> dict:
    keys = jax.random.split(jax.random.key(seed), 16)
    features = centred(keys[0], (DOMX, DOMY, A_DEV, H), 1.0, 6.0, ((0, 8), (1, 32)))
    displacement = draw_displacement(jax.random.fold_in(keys[15], 71), 0)
    neighbours = draw_neighbours(jax.random.fold_in(keys[15], 71), 0)
    neighbour_count = draw_neighbour_count(jax.random.fold_in(keys[15], 71), 0)
    species = set_ends(jax.random.randint(keys[4], (DOMX, DOMY, A_DEV), 0, NSPEC), jax.random.fold_in(keys[4], 1), 0, NSPEC - 1).astype(jnp.int32)
    send_list = draw_send_list(jax.random.fold_in(keys[15], 71), 0)
    send_count = draw_send_count(jax.random.fold_in(keys[15], 71), 0)
    w_center = centred(keys[7], (H, HID), H ** -0.5, 0.375)
    w_neighbour = centred(keys[8], (H, HID), H ** -0.5, 0.375)
    w_radial = centred(keys[9], (NB, HID), 2 ** -0.5, 4.0)
    w_hidden = centred(keys[10], (HID, HID), HID ** -0.5, 0.1875)
    w_tensor = centred(keys[11], (HID, CH), HID ** -0.5, 0.1875)
    readout = centred(keys[12], (CH,), (4 * CH) ** -0.5, 0.375, (), jnp.float32)
    species_scale = jnp.clip(jnp.exp(jax.random.uniform(keys[13], (NSPEC,), jnp.float32, math.log(0.5), math.log(2.0))), 0.5, 2.0)
    species_shift = centred(keys[14], (NSPEC,), 1.0, 4.0, (), jnp.float32)
    return dict(features=features, displacement=displacement, neighbours=neighbours, neighbour_count=neighbour_count, species=species, send_list=send_list, send_count=send_count, w_center=w_center, w_neighbour=w_neighbour, w_radial=w_radial, w_hidden=w_hidden, w_tensor=w_tensor, readout=readout, species_scale=species_scale, species_shift=species_shift)


DIRECTIONS = ((-1, -1), (-1, 0), (-1, 1), (0, -1), (0, 1), (1, -1), (1, 0), (1, 1))

def atom_energies(displace, centre_proj, table_proj, table_rows, neighbour_ids, live_mask, scale_atom, shift_atom, w_radial, w_hidden, w_tensor, readout):
    edge_total = displace.shape[1]
    atom_total = centre_proj.shape[0]
    per_atom = edge_total // atom_total
    channels = w_tensor.shape[1]
    basis_count = w_radial.shape[0]
    squared = lax.optimization_barrier(jnp.sum(displace * displace, axis=0))
    distance = jnp.sqrt(squared)
    unit_vec = displace / distance[None, :]
    centres = (jnp.arange(basis_count).astype(jnp.float32) + 1.0) / basis_count
    basis_rows = jnp.exp(-jnp.square((distance[None, :] - centres[:, None]) * (0.5 * basis_count))).astype(jnp.bfloat16)
    radial = lax.dot_general(basis_rows, w_radial, (((0,), (0,)), ((), ())), preferred_element_type=jnp.float32)
    centre_rows = jnp.broadcast_to(centre_proj[:, None, :], (atom_total, per_atom, centre_proj.shape[1])).reshape(edge_total, centre_proj.shape[1])
    pre_act = centre_rows.astype(jnp.float32) + jnp.take(table_proj, neighbour_ids, axis=0).astype(jnp.float32) + radial
    first_layer = jax.nn.silu(pre_act).astype(jnp.bfloat16)
    second_layer = jax.nn.silu(jnp.dot(first_layer, w_hidden, preferred_element_type=jnp.float32)).astype(jnp.bfloat16)
    tensor_wts = jnp.dot(second_layer, w_tensor, preferred_element_type=jnp.float32)
    gathered = jnp.take(table_rows, neighbour_ids, axis=0).astype(jnp.float32)
    scalar_part = gathered[:, :channels]
    vector_parts = [gathered[:, channels * (axis_num + 1):channels * (axis_num + 2)] for axis_num in range(3)]
    envelope = jnp.square(1.0 - squared) * live_mask
    weighted = tensor_wts * envelope[:, None]
    along_unit = unit_vec[0][:, None] * vector_parts[0] + unit_vec[1][:, None] * vector_parts[1] + unit_vec[2][:, None] * vector_parts[2]
    pieces = [weighted * (scalar_part + along_unit)]
    for axis_num in range(3):
        pieces.append(weighted * (scalar_part * unit_vec[axis_num][:, None] + vector_parts[axis_num]))
    invariant = jnp.zeros((atom_total, channels), jnp.float32)
    for member in pieces:
        invariant = invariant + jnp.square(member.reshape(atom_total, per_atom, channels).sum(axis=1))
    return scale_atom * lax.optimization_barrier(jnp.sum(invariant * readout[None, :], axis=1)) + shift_atom

def domain_terms(own_rows, ghost_rows, displace, neighbour_ids, live_count, species_ids, w_center, w_neighbour, w_radial, w_hidden, w_tensor, readout, species_scale, species_shift):
    atom_total, row_width = own_rows.shape
    per_atom = displace.shape[1] // atom_total
    slot_count = ghost_rows.shape[1]
    table_rows = jnp.concatenate([own_rows, ghost_rows.reshape(8 * slot_count, row_width)], axis=0)
    centre_proj = jnp.dot(own_rows, w_center, preferred_element_type=jnp.float32).astype(jnp.bfloat16)
    table_proj = jnp.dot(table_rows, w_neighbour, preferred_element_type=jnp.float32).astype(jnp.bfloat16)
    live_mask = (jnp.arange(per_atom)[None, :] < live_count[:, None]).astype(jnp.float32).reshape(-1)
    species_hit = jnp.arange(species_scale.shape[0])[None, :] == species_ids[:, None]
    scale_atom = lax.optimization_barrier(jnp.sum(jnp.where(species_hit, species_scale[None, :], 0.0), axis=1))
    shift_atom = lax.optimization_barrier(jnp.sum(jnp.where(species_hit, species_shift[None, :], 0.0), axis=1))

    def energy_of(displaced):
        return atom_energies(displaced, centre_proj, table_proj, table_rows, neighbour_ids, live_mask, scale_atom, shift_atom, w_radial, w_hidden, w_tensor, readout)
    energy, pullback = jax.vjp(energy_of, displace)
    edge_grad = pullback(jnp.ones_like(energy))[0]
    own_force = edge_grad.reshape(3, atom_total, per_atom).sum(axis=2)
    row_force = jax.ops.segment_sum(edge_grad.T, neighbour_ids, num_segments=atom_total + 8 * slot_count)
    own_force = own_force - row_force[:atom_total].T
    ghost_force = row_force[atom_total:].reshape(8, slot_count, 3).transpose(0, 2, 1)
    return (energy, own_force, ghost_force)

def scatter_block(block_force, atom_ids, atom_total):
    return jax.ops.segment_sum(block_force.T, atom_ids, num_segments=atom_total).T

def reference(features, displacement, neighbours, neighbour_count, species, send_list, send_count, w_center, w_neighbour, w_radial, w_hidden, w_tensor, readout, species_scale, species_shift):
    dom_x, dom_y, atom_total = (features.shape[0], features.shape[1], features.shape[2])

    def ghosts_of(pos_x, pos_y):
        blocks = []
        for direction, offset in enumerate(DIRECTIONS):
            sender_x = (pos_x + offset[0]) % dom_x
            sender_y = (pos_y + offset[1]) % dom_y
            atom_ids = send_list[sender_x, sender_y, 7 - direction]
            limit = send_count[sender_x, sender_y, 7 - direction]
            picked = jnp.take(features[sender_x, sender_y], atom_ids, axis=0)
            keeping = jnp.arange(atom_ids.shape[0]) < limit
            blocks.append(jnp.where(keeping[:, None], picked, jnp.zeros_like(picked)))
        return jnp.stack(blocks)

    def per_domain(flat_id):
        pos_x = flat_id // dom_y
        pos_y = flat_id % dom_y
        return domain_terms(features[pos_x, pos_y], ghosts_of(pos_x, pos_y), displacement[pos_x, pos_y], neighbours[pos_x, pos_y], neighbour_count[pos_x, pos_y], species[pos_x, pos_y], w_center, w_neighbour, w_radial, w_hidden, w_tensor, readout, species_scale, species_shift)
    energy, own_force, ghost_force = lax.map(per_domain, jnp.arange(dom_x * dom_y).astype(jnp.int32))
    energy = energy.reshape(dom_x, dom_y, atom_total)
    forces = own_force.reshape(dom_x, dom_y, 3, atom_total)
    ghost_force = ghost_force.reshape(dom_x, dom_y, 8, 3, -1)
    scatter_all = jax.vmap(jax.vmap(lambda block_force, atom_ids: scatter_block(block_force, atom_ids, atom_total)))
    for direction, offset in enumerate(DIRECTIONS):
        incoming = jnp.roll(ghost_force[:, :, 7 - direction], (-offset[0], -offset[1]), (0, 1))
        forces = forces + scatter_all(incoming, send_list[:, :, direction])
    return (energy, forces)
```

```python
import jax
import jax.numpy as jnp
from jax import lax
from jax.experimental import pallas as pl
from jax.experimental.pallas import tpu as pltpu
from jax.sharding import PartitionSpec as P

DIRECTIONS = ((-1, -1), (-1, 0), (-1, 1), (0, -1), (0, 1), (1, -1), (1, 0), (1, 1))
ATOMS = 256
SLOTS = 8
EDGES = ATOMS * SLOTS
GHOSTS = 192
WIDTH = 256
HID = 1024
CH = 64
F32 = jnp.float32
BF16 = jnp.bfloat16
MESH = pl.DeviceIdType.MESH


def iota(shape, dim):
    return lax.broadcasted_iota(jnp.int32, shape, dim)


def one_hot(hit):
    return jnp.where(hit, 1.0, 0.0).astype(BF16)


def dot(a, b):
    return jnp.dot(a, b, preferred_element_type=F32)


def silu_pair(value):
    gate = 0.5 * jnp.tanh(0.5 * value) + 0.5
    act = value * gate
    return act, gate + act * (1.0 - gate)


def split(value):
    high = value.astype(BF16)
    return high, (value - high.astype(F32)).astype(BF16)


def kernel(
    feat,
    disp,
    nbr,
    cnt,
    spc,
    lists,
    scnt,
    wc_hbm,
    wn_hbm,
    wr,
    wh_hbm,
    wt_hbm,
    ro,
    sscale,
    sshift,
    en_ref,
    fo_ref,
    wc,
    wn,
    wh,
    wt,
    wct,
    wnt,
    wrt,
    wht,
    wtt,
    sel,
    outg,
    ghost,
    tg,
    stage,
    dsp,
    geo,
    oh,
    pre,
    drad,
    rows,
    act1,
    act2,
    tws,
    grads,
    back_out,
    back_in,
    load_sem,
    send_sem,
    recv_sem,
    bsend_sem,
    brecv_sem,
):
    px, qy = lax.axis_index("gx"), lax.axis_index("gy")
    nx, ny = lax.axis_size("gx"), lax.axis_size("gy")
    peers = [
        (lax.rem(px + (ox + nx), nx), lax.rem(qy + (oy + ny), ny)) for ox, oy in DIRECTIONS
    ]
    loads = [
        pltpu.make_async_copy(src, dst, load_sem.at[num])
        for num, (src, dst) in enumerate(
            ((wc_hbm, wc), (wn_hbm, wn), (wh_hbm, wh), (wt_hbm, wt))
        )
    ]
    for load in loads:
        load.start()
    barrier = pltpu.get_barrier_semaphore()
    for peer in peers:
        pl.semaphore_signal(barrier, inc=1, device_id=peer, device_id_type=MESH)

    kept = jnp.where(
        iota((GHOSTS, 8), 0) < scnt[...], jnp.transpose(lists[...].astype(F32)), -1.0
    )
    lane = iota((GHOSTS, ATOMS), 1).astype(F32)
    for num in range(8):
        hit = one_hot(kept[:, num : num + 1] == lane)
        sel[num] = hit
        outg[num] = dot(hit, feat[...]).astype(BF16)
    pl.semaphore_wait(barrier, 8)
    sends = []
    for num in range(8):
        copy = pltpu.make_async_remote_copy(
            src_ref=outg.at[num],
            dst_ref=ghost.at[7 - num],
            send_sem=send_sem.at[num],
            recv_sem=recv_sem.at[7 - num],
            device_id=peers[num],
            device_id_type=MESH,
        )
        copy.start()
        sends.append(copy)

    for axis in range(3):
        for c in range(16):
            stage[pl.ds(axis * 16 + c, 1), :] = disp[axis : axis + 1, c * 128 : (c + 1) * 128]
    for c in range(16):
        stage[pl.ds(48 + c, 1), :] = nbr[0:1, c * 128 : (c + 1) * 128].astype(F32)
    turned = jnp.transpose(stage[...])
    for row in range(4):
        for a in range(16):
            dsp[row, :, a * 16 : (a + 1) * 16] = turned[
                a * 8 : (a + 1) * 8, row * 16 : (row + 1) * 16
            ]
    col = iota((ATOMS, ATOMS), 1)
    swap = iota((ATOMS, ATOMS), 0) == (col & 15) * 16 + (col >> 4)
    swap_b = one_hot(swap)
    small = jnp.concatenate(
        [cnt[...].astype(F32), spc[...].astype(F32), jnp.zeros((14, ATOMS), F32)], axis=0
    ).astype(BF16)
    small = dot(small, swap_b)
    count, kind = small[0:1], small[1:2]
    scale = jnp.zeros((1, ATOMS), F32)
    shift = jnp.zeros((1, ATOMS), F32)
    for num in range(4):
        hit = kind == float(num)
        scale = jnp.where(hit, sscale[0:1, num : num + 1], scale)
        shift = jnp.where(hit, sshift[0:1, num : num + 1], shift)
    squared = dsp[0] * dsp[0] + dsp[1] * dsp[1] + dsp[2] * dsp[2]
    distance = jnp.sqrt(squared)
    inverse = 1.0 / distance
    live = jnp.where(iota((SLOTS, ATOMS), 0).astype(F32) < count, 1.0, 0.0)
    for axis in range(3):
        geo[axis] = dsp[axis] * inverse
    geo[3] = jnp.square(1.0 - squared) * live
    geo[4] = distance
    geo[5] = -4.0 * (1.0 - squared) * live
    geo[6] = inverse

    wrt[...] = jnp.transpose(
        jnp.concatenate([wr[...].astype(F32), jnp.zeros((120, HID), F32)], axis=0)
    ).astype(BF16)
    loads[0].wait()
    for num in range(4):
        wct[num * 256 : (num + 1) * 256, :] = jnp.transpose(wc[:, num * 256 : (num + 1) * 256])
    loads[1].wait()
    for num in range(4):
        wnt[num * 256 : (num + 1) * 256, :] = jnp.transpose(wn[:, num * 256 : (num + 1) * 256])
    loads[2].wait()

    def turn(num, carry):
        start = pl.multiple_of(num * 256, 256)
        for part in range(4):
            wht[pl.ds(start, 256), part * 256 : (part + 1) * 256] = jnp.transpose(
                wh[part * 256 : (part + 1) * 256, pl.ds(start, 256)]
            )
        return carry

    lax.fori_loop(0, 4, turn, 0)
    loads[3].wait()
    for part in range(4):
        wtt[:, part * 256 : (part + 1) * 256] = jnp.transpose(wt[part * 256 : (part + 1) * 256, :])

    feat_t = jnp.transpose(feat[...])
    feat_p = dot(feat_t, swap_b).astype(BF16)
    unit_id = iota((16, ATOMS), 0)
    centre_at = (unit_id.astype(F32) + 1.0) * 0.125
    row_id = iota((256, ATOMS), 0).astype(F32)

    def before(k, carry):
        lanes = pl.ds(pl.multiple_of(k * 256, 256), 256)
        ids = dsp[3, pl.ds(k, 1), :]
        for part in range(7):
            oh[part * 256 : (part + 1) * 256, lanes] = one_hot(row_id + (part * 256.0) == ids)
        rows[:, lanes] = dot(feat_t, oh[0:256, lanes]).astype(BF16)
        offset = (geo[4, pl.ds(k, 1), :] - centre_at) * 4.0
        basis = jnp.where(unit_id < 8, jnp.exp(-offset * offset), 0.0)
        both = jnp.concatenate([basis, -8.0 * offset * basis], axis=1).astype(BF16)
        both = jnp.concatenate([both, jnp.zeros((112, 512), BF16)], axis=0)
        for part in range(4):
            here = slice(part * 256, (part + 1) * 256)
            radial = dot(wrt[here, :], both)
            pre[k, here, :] = radial[:, :256] + dot(wct[here, :], feat_p)
            drad[k, here, :] = radial[:, 256:]
        return carry

    lax.fori_loop(0, SLOTS, before, 0)

    for num in range(8):
        sends[num].wait_send()
        sends[7 - num].wait_recv()
    for pair in range(4):
        tg[:, pair * 2 * GHOSTS : (pair + 1) * 2 * GHOSTS] = jnp.transpose(
            jnp.concatenate([ghost[2 * pair], ghost[2 * pair + 1]], axis=0)
        )

    def mlp(k, sums):
        lanes = pl.ds(pl.multiple_of(k * 256, 256), 256)
        found = dot(tg[...], oh[256:1792, lanes]).astype(BF16) + rows[:, lanes]
        rows[:, lanes] = found
        for part in range(4):
            here = slice(part * 256, (part + 1) * 256)
            act, slope = silu_pair(dot(wnt[here, :], found) + pre[k, here, :])
            act1[here, 0:256] = act.astype(BF16)
            act1[here, 256:512] = (slope * drad[k, here, :]).astype(BF16)
        for part in range(4):
            here = slice(part * 256, (part + 1) * 256)
            hidden = dot(wht[here, :], act1[...])
            act, slope = silu_pair(hidden[:, :256])
            act2[here, 0:256] = act.astype(BF16)
            act2[here, 256:512] = (slope * hidden[:, 256:]).astype(BF16)
        weight = dot(wtt[...], act2[...])
        tws[k] = weight
        unit = [geo[axis, pl.ds(k, 1), :] for axis in range(3)]
        row = found.astype(F32)
        s, v = row[0:CH], [row[CH * (m + 1) : CH * (m + 2)] for m in range(3)]
        w = weight[:, :256] * geo[3, pl.ds(k, 1), :]
        out = [sums[0] + w * (s + unit[0] * v[0] + unit[1] * v[1] + unit[2] * v[2])]
        for m in range(3):
            out.append(sums[m + 1] + w * (s * unit[m] + v[m]))
        return tuple(out)

    sums = lax.fori_loop(
        0, SLOTS, mlp, tuple(jnp.zeros((CH, ATOMS), F32) for _ in range(4))
    )

    eye = iota((CH, CH), 0) == iota((CH, CH), 1)
    read = jnp.sum(jnp.where(eye, ro[...], 0.0), axis=1, keepdims=True)
    inv = sums[0] * sums[0] + sums[1] * sums[1] + sums[2] * sums[2] + sums[3] * sums[3]
    energy = scale * jnp.sum(inv * read, axis=0, keepdims=True) + shift
    factor = 2.0 * scale * read
    cot = [factor * total for total in sums]

    def slopes(k, own):
        lanes = pl.ds(pl.multiple_of(k * 256, 256), 256)
        unit = [geo[axis, pl.ds(k, 1), :] for axis in range(3)]
        env = geo[3, pl.ds(k, 1), :]
        row = rows[:, lanes].astype(F32)
        s, v = row[0:CH], [row[CH * (m + 1) : CH * (m + 2)] for m in range(3)]
        weight = tws[k]
        tw, dtw = weight[:, :256], weight[:, 256:]
        q = cot[0] * (s + unit[0] * v[0] + unit[1] * v[1] + unit[2] * v[2])
        for m in range(3):
            q = q + cot[m + 1] * (s * unit[m] + v[m])
        by_dist = env * jnp.sum(q * dtw, axis=0, keepdims=True)
        by_env = jnp.sum(q * tw, axis=0, keepdims=True)
        w = tw * env
        by_unit = [
            jnp.sum(w * (cot[0] * v[m] + cot[m + 1] * s), axis=0, keepdims=True) for m in range(3)
        ]
        along = by_unit[0] * unit[0] + by_unit[1] * unit[1] + by_unit[2] * unit[2]
        inverse_k = geo[6, pl.ds(k, 1), :]
        common = by_dist - along * inverse_k
        scaled = by_env * geo[5, pl.ds(k, 1), :]
        grad = jnp.concatenate(
            [
                common * unit[m] + scaled * dsp[m, pl.ds(k, 1), :] + by_unit[m] * inverse_k
                for m in range(3)
            ]
            + [jnp.zeros((5, ATOMS), F32)],
            axis=0,
        )
        high, low = split(grad)
        grads[0:8, lanes] = high
        grads[8:16, lanes] = low
        return own + grad

    own = lax.fori_loop(0, SLOTS, slopes, jnp.zeros((8, ATOMS), F32))

    def scatter(first, size):
        both = lax.dot_general(
            grads[...],
            oh[first : first + size, :],
            (((1,), (1,)), ((), ())),
            preferred_element_type=F32,
        )
        return both[0:8] + both[8:16]

    returns = []
    for num in range(8):
        back_out[num] = scatter(ATOMS + num * GHOSTS, GHOSTS)
        copy = pltpu.make_async_remote_copy(
            src_ref=back_out.at[num],
            dst_ref=back_in.at[7 - num],
            send_sem=bsend_sem.at[num],
            recv_sem=brecv_sem.at[7 - num],
            device_id=peers[num],
            device_id_type=MESH,
        )
        copy.start()
        returns.append(copy)
    tail = jnp.concatenate([own[0:3], energy, jnp.zeros((4, ATOMS), F32)], axis=0)
    tail = jnp.dot(
        tail, jnp.where(swap, 1.0, 0.0), preferred_element_type=F32, precision=lax.Precision.HIGHEST
    )
    en_ref[...] = tail[3:4]
    total = tail[0:3] - scatter(0, ATOMS)[0:3]
    for num in range(8):
        returns[num].wait_send()
        returns[7 - num].wait_recv()
    for num in range(8):
        high, low = split(back_in[num])
        landed = dot(jnp.concatenate([high, low], axis=0), sel[num])
        total = total + landed[0:3] + landed[8:11]
    fo_ref[...] = total


def shards(
    features,
    displacement,
    neighbours,
    neighbour_count,
    species,
    send_list,
    send_count,
    w_center,
    w_neighbour,
    w_radial,
    w_hidden,
    w_tensor,
    readout,
    species_scale,
    species_shift,
):
    vmem = pl.BlockSpec(memory_space=pltpu.VMEM)
    hbm = pl.BlockSpec(memory_space=pl.ANY)
    energy, forces = pl.pallas_call(
        kernel,
        out_shape=(
            jax.ShapeDtypeStruct((1, ATOMS), F32),
            jax.ShapeDtypeStruct((3, ATOMS), F32),
        ),
        in_specs=[vmem] * 7 + [hbm, hbm, vmem, hbm, hbm] + [vmem] * 3,
        out_specs=(vmem, vmem),
        scratch_shapes=[
            pltpu.VMEM((WIDTH, HID), BF16),
            pltpu.VMEM((WIDTH, HID), BF16),
            pltpu.VMEM((HID, HID), BF16),
            pltpu.VMEM((HID, CH), BF16),
            pltpu.VMEM((HID, WIDTH), BF16),
            pltpu.VMEM((HID, WIDTH), BF16),
            pltpu.VMEM((HID, 128), BF16),
            pltpu.VMEM((HID, HID), BF16),
            pltpu.VMEM((CH, HID), BF16),
            pltpu.VMEM((8, GHOSTS, ATOMS), BF16),
            pltpu.VMEM((8, GHOSTS, WIDTH), BF16),
            pltpu.VMEM((8, GHOSTS, WIDTH), BF16),
            pltpu.VMEM((WIDTH, 8 * GHOSTS), BF16),
            pltpu.VMEM((64, 128), F32),
            pltpu.VMEM((4, SLOTS, ATOMS), F32),
            pltpu.VMEM((7, SLOTS, ATOMS), F32),
            pltpu.VMEM((ATOMS + 8 * GHOSTS, EDGES), BF16),
            pltpu.VMEM((SLOTS, HID, ATOMS), F32),
            pltpu.VMEM((SLOTS, HID, ATOMS), F32),
            pltpu.VMEM((WIDTH, EDGES), BF16),
            pltpu.VMEM((HID, 2 * ATOMS), BF16),
            pltpu.VMEM((HID, 2 * ATOMS), BF16),
            pltpu.VMEM((SLOTS, CH, 2 * ATOMS), F32),
            pltpu.VMEM((16, EDGES), BF16),
            pltpu.VMEM((8, 8, GHOSTS), F32),
            pltpu.VMEM((8, 8, GHOSTS), F32),
            pltpu.SemaphoreType.DMA((4,)),
            pltpu.SemaphoreType.DMA((8,)),
            pltpu.SemaphoreType.DMA((8,)),
            pltpu.SemaphoreType.DMA((8,)),
            pltpu.SemaphoreType.DMA((8,)),
        ],
        compiler_params=pltpu.CompilerParams(
            collective_id=0, has_side_effects=True, vmem_limit_bytes=56 * 1024 * 1024
        ),
        cost_estimate=pl.CostEstimate(
            flops=14_000_000_000, bytes_accessed=4_000_000, transcendentals=4_000_000
        ),
    )(
        features[0, 0],
        displacement[0, 0],
        neighbours[0],
        neighbour_count[0],
        species[0],
        send_list[0, 0],
        send_count[0],
        w_center,
        w_neighbour,
        w_radial,
        w_hidden,
        w_tensor,
        readout[None],
        species_scale[None],
        species_shift[None],
    )
    return energy[None], forces[None, None]


def solution(mesh):
    placed = (
        P("gx", "gy", None, None),
        P("gx", "gy", None, None),
        P("gx", "gy", None),
        P("gx", "gy", None),
        P("gx", "gy", None),
        P("gx", "gy", None, None),
        P("gx", "gy", None),
        P(),
        P(),
        P(),
        P(),
        P(),
        P(),
        P(),
        P(),
    )
    return jax.shard_map(
        shards,
        mesh=mesh,
        in_specs=placed,
        out_specs=(P("gx", "gy", None), P("gx", "gy", None, None)),
        check_vma=False,
    )
```

```python
import jax
import jax.numpy as jnp
from jax import lax
from jax.experimental import pallas as pl
from jax.experimental.pallas import tpu as pltpu
from jax.sharding import PartitionSpec as P

DIRECTIONS = ((-1, -1), (-1, 0), (-1, 1), (0, -1), (0, 1), (1, -1), (1, 0), (1, 1))
ATOMS = 256
SLOTS = 8
EDGES = ATOMS * SLOTS
GHOSTS = 192
WIDTH = 256
HID = 1024
CH = 64
F32 = jnp.float32
BF16 = jnp.bfloat16
MESH = pl.DeviceIdType.MESH


def iota(shape, dim):
    return lax.broadcasted_iota(jnp.int32, shape, dim)


def one_hot(hit):
    return jnp.where(hit, 1.0, 0.0).astype(BF16)


def dot(a, b):
    return jnp.dot(a, b, preferred_element_type=F32)


def silu_pair(value):
    gate = 0.5 * jnp.tanh(0.5 * value) + 0.5
    act = value * gate
    return act, gate + act * (1.0 - gate)


def split(value):
    high = value.astype(BF16)
    return high, (value - high.astype(F32)).astype(BF16)


def kernel(
    feat,
    disp,
    nbr,
    cnt,
    spc,
    lists,
    scnt,
    wc_hbm,
    wn_hbm,
    wr,
    wh_hbm,
    wtt_hbm,
    ro,
    sscale,
    sshift,
    out_ref,
    wc,
    wn,
    wh,
    wct,
    wnt,
    wrt,
    wht,
    wtt,
    sel,
    outg,
    ghost,
    stage,
    dsp,
    geo,
    oh,
    pre,
    drad,
    rows,
    act1,
    act2,
    tws,
    back_out,
    back_in,
    load_sem,
    send_sem,
    recv_sem,
    bsend_sem,
    brecv_sem,
):
    px, qy = lax.axis_index("gx"), lax.axis_index("gy")
    nx, ny = lax.axis_size("gx"), lax.axis_size("gy")

    def peer(ox, oy):
        return lax.rem(px + (ox + nx), nx), lax.rem(qy + (oy + ny), ny)

    core = lax.rem(qy, 2)
    side = 2 * core - 1
    order = [
        (6 + side, peer(1, side)),
        (1 + side, peer(-1, side)),
        (3 + core, peer(0, side)),
        (6 - side, peer(1, -side)),
        (1 - side, peer(-1, -side)),
        (6, peer(1, 0)),
        (1, peer(-1, 0)),
        (4 - core, peer(0, -side)),
    ]
    loads = [
        pltpu.make_async_copy(src, dst, load_sem.at[num])
        for num, (src, dst) in enumerate(
            ((wc_hbm, wc), (wn_hbm, wn), (wh_hbm, wh), (wtt_hbm, wtt))
        )
    ]
    for load in loads:
        load.start()
    barrier = pltpu.get_barrier_semaphore()
    for _, device in order:
        pl.semaphore_signal(barrier, inc=1, device_id=device, device_id_type=MESH)

    kept = jnp.where(
        iota((GHOSTS, 8), 0) < scnt[...], jnp.transpose(lists[...].astype(F32)), -1.0
    )
    lane = iota((GHOSTS, ATOMS), 1).astype(F32)
    for num in range(8):
        hit = one_hot(kept[:, num : num + 1] == lane)
        sel[num] = hit
        outg[num] = dot(hit, feat[...]).astype(BF16)
    pl.semaphore_wait(barrier, 8)
    sends = []
    for num, peer in order:
        copy = pltpu.make_async_remote_copy(
            src_ref=outg.at[num],
            dst_ref=ghost.at[7 - num],
            send_sem=send_sem.at[num],
            recv_sem=recv_sem.at[7 - num],
            device_id=peer,
            device_id_type=MESH,
        )
        copy.start()
        sends.append(copy)

    for axis in range(3):
        for c in range(16):
            stage[pl.ds(axis * 16 + c, 1), :] = disp[axis, :, c * 128 : (c + 1) * 128]
    for c in range(16):
        stage[pl.ds(48 + c, 1), :] = nbr[0:1, c * 128 : (c + 1) * 128].astype(F32)
    turned = jnp.transpose(stage[...])
    for row in range(4):
        for a in range(16):
            dsp[row, :, a * 16 : (a + 1) * 16] = turned[
                a * 8 : (a + 1) * 8, row * 16 : (row + 1) * 16
            ]
    col = iota((ATOMS, ATOMS), 1)
    swap = iota((ATOMS, ATOMS), 0) == (col & 15) * 16 + (col >> 4)
    swap_b = one_hot(swap)
    small = jnp.concatenate(
        [cnt[...].astype(F32), spc[...].astype(F32), jnp.zeros((14, ATOMS), F32)], axis=0
    ).astype(BF16)
    small = dot(small, swap_b)
    count, kind = small[0:1], small[1:2]
    scale = jnp.zeros((1, ATOMS), F32)
    shift = jnp.zeros((1, ATOMS), F32)
    for num in range(4):
        hit = kind == float(num)
        scale = jnp.where(hit, sscale[0:1, num : num + 1], scale)
        shift = jnp.where(hit, sshift[0:1, num : num + 1], shift)
    squared = dsp[0] * dsp[0] + dsp[1] * dsp[1] + dsp[2] * dsp[2]
    distance = jnp.sqrt(squared)
    inverse = 1.0 / distance
    live = jnp.where(iota((SLOTS, ATOMS), 0).astype(F32) < count, 1.0, 0.0)
    for axis in range(3):
        geo[axis] = dsp[axis] * inverse
    geo[3] = jnp.square(1.0 - squared) * live
    geo[4] = distance
    geo[5] = -4.0 * (1.0 - squared) * live
    geo[6] = inverse

    wrt[...] = jnp.transpose(
        jnp.concatenate([wr[...].astype(F32), jnp.zeros((120, HID), F32)], axis=0)
    ).astype(BF16)
    loads[0].wait()
    for num in range(4):
        wct[num * 256 : (num + 1) * 256, :] = jnp.transpose(wc[:, num * 256 : (num + 1) * 256])
    loads[1].wait()
    for num in range(4):
        wnt[num * 256 : (num + 1) * 256, :] = jnp.transpose(wn[:, num * 256 : (num + 1) * 256])
    loads[2].wait()

    def turn(num, carry):
        start = pl.multiple_of(num * 256, 256)
        for part in range(4):
            wht[pl.ds(start, 256), part * 256 : (part + 1) * 256] = jnp.transpose(
                wh[part * 256 : (part + 1) * 256, pl.ds(start, 256)]
            )
        return carry

    lax.fori_loop(0, 4, turn, 0)
    loads[3].wait()

    feat_t = jnp.transpose(feat[...])
    feat_p = dot(feat_t, swap_b).astype(BF16)
    unit_id = iota((16, ATOMS), 0)
    centre_at = (unit_id.astype(F32) + 1.0) * 0.125
    row_id = iota((256, ATOMS), 0).astype(F32)

    def before(k, carry):
        lanes = pl.ds(pl.multiple_of(k * 256, 256), 256)
        ids = dsp[3, pl.ds(k, 1), :]
        for part in range(7):
            oh[part * 256 : (part + 1) * 256, lanes] = one_hot(row_id + (part * 256.0) == ids)
        rows[:, lanes] = dot(feat_t, oh[0:256, lanes]).astype(BF16)
        offset = (geo[4, pl.ds(k, 1), :] - centre_at) * 4.0
        basis = jnp.where(unit_id < 8, jnp.exp(-offset * offset), 0.0)
        both = jnp.concatenate([basis, -8.0 * offset * basis], axis=1).astype(BF16)
        both = jnp.concatenate([both, jnp.zeros((112, 512), BF16)], axis=0)
        for part in range(4):
            here = slice(part * 256, (part + 1) * 256)
            radial = dot(wrt[here, :], both)
            pre[k, here, :] = radial[:, :256] + dot(wct[here, :], feat_p)
            drad[k, here, :] = radial[:, 256:]
        return carry

    lax.fori_loop(0, SLOTS, before, 0)

    def take(num):
        turned = jnp.transpose(ghost[num])
        first = pl.multiple_of(ATOMS + num * GHOSTS, 64)
        for part in range(4):
            here = slice(part * 512, (part + 1) * 512)
            found = dot(turned, oh[pl.ds(first, GHOSTS), here])
            rows[:, here] = rows[:, here] + found.astype(BF16)

    for copy in sends:
        copy.wait_send()
    for copy in (2, 5, 6, 1, 0, 7, 4, 3):
        sends[copy].wait_recv()
        take(7 - order[copy][0])

    def mlp(k, sums):
        lanes = slice(k * 256, (k + 1) * 256)
        found = rows[:, lanes]
        for part in range(4):
            here = slice(part * 256, (part + 1) * 256)
            act, slope = silu_pair(dot(wnt[here, :], found) + pre[k, here, :])
            act1[here, 0:256] = act.astype(BF16)
            act1[here, 256:512] = (slope * drad[k, here, :]).astype(BF16)
        for part in range(4):
            here = slice(part * 256, (part + 1) * 256)
            hidden = dot(wht[here, :], act1[...])
            act, slope = silu_pair(hidden[:, :256])
            act2[here, 0:256] = act.astype(BF16)
            act2[here, 256:512] = (slope * hidden[:, 256:]).astype(BF16)
        weight = dot(wtt[...], act2[...])
        tws[k] = weight
        unit = [geo[axis, pl.ds(k, 1), :] for axis in range(3)]
        row = found.astype(F32)
        s, v = row[0:CH], [row[CH * (m + 1) : CH * (m + 2)] for m in range(3)]
        w = weight[:, :256] * geo[3, pl.ds(k, 1), :]
        out = [sums[0] + w * (s + unit[0] * v[0] + unit[1] * v[1] + unit[2] * v[2])]
        for m in range(3):
            out.append(sums[m + 1] + w * (s * unit[m] + v[m]))
        return tuple(out)

    sums = tuple(jnp.zeros((CH, ATOMS), F32) for _ in range(4))
    for k in range(SLOTS):
        sums = mlp(k, sums)

    eye = iota((CH, CH), 0) == iota((CH, CH), 1)
    read = jnp.sum(jnp.where(eye, ro[...], 0.0), axis=1, keepdims=True)
    inv = sums[0] * sums[0] + sums[1] * sums[1] + sums[2] * sums[2] + sums[3] * sums[3]
    energy = scale * jnp.sum(inv * read, axis=0, keepdims=True) + shift
    factor = 2.0 * scale * read
    cot = [factor * total for total in sums]

    def slopes(k, own, landed):
        lanes = slice(k * 256, (k + 1) * 256)
        unit = [geo[axis, pl.ds(k, 1), :] for axis in range(3)]
        env = geo[3, pl.ds(k, 1), :]
        row = rows[:, lanes].astype(F32)
        s, v = row[0:CH], [row[CH * (m + 1) : CH * (m + 2)] for m in range(3)]
        weight = tws[k]
        tw, dtw = weight[:, :256], weight[:, 256:]
        q = cot[0] * (s + unit[0] * v[0] + unit[1] * v[1] + unit[2] * v[2])
        for m in range(3):
            q = q + cot[m + 1] * (s * unit[m] + v[m])
        by_dist = env * jnp.sum(q * dtw, axis=0, keepdims=True)
        by_env = jnp.sum(q * tw, axis=0, keepdims=True)
        w = tw * env
        by_unit = [
            jnp.sum(w * (cot[0] * v[m] + cot[m + 1] * s), axis=0, keepdims=True) for m in range(3)
        ]
        along = by_unit[0] * unit[0] + by_unit[1] * unit[1] + by_unit[2] * unit[2]
        inverse_k = geo[6, pl.ds(k, 1), :]
        common = by_dist - along * inverse_k
        scaled = by_env * geo[5, pl.ds(k, 1), :]
        grad = jnp.concatenate(
            [
                common * unit[m] + scaled * dsp[m, pl.ds(k, 1), :] + by_unit[m] * inverse_k
                for m in range(3)
            ]
            + [jnp.zeros((5, ATOMS), F32)],
            axis=0,
        )
        spread = lax.dot_general(
            jnp.concatenate(split(grad), axis=0),
            oh[:, lanes],
            (((1,), (1,)), ((), ())),
            preferred_element_type=F32,
        )
        return own + grad, landed + spread

    own = jnp.zeros((8, ATOMS), F32)
    landed = jnp.zeros((16, ATOMS + 8 * GHOSTS), F32)
    for k in range(SLOTS):
        own, landed = slopes(k, own, landed)
    landed = landed[0:8] + landed[8:16]

    for num in range(8):
        back_out[num] = landed[:, ATOMS + num * GHOSTS : ATOMS + (num + 1) * GHOSTS]
    returns = []
    for num, device in order:
        copy = pltpu.make_async_remote_copy(
            src_ref=back_out.at[num],
            dst_ref=back_in.at[7 - num],
            send_sem=bsend_sem.at[num],
            recv_sem=brecv_sem.at[7 - num],
            device_id=device,
            device_id_type=MESH,
        )
        copy.start()
        returns.append(copy)
    tail = jnp.concatenate([own[0:3], energy, jnp.zeros((4, ATOMS), F32)], axis=0)
    tail = jnp.dot(
        tail, jnp.where(swap, 1.0, 0.0), preferred_element_type=F32, precision=lax.Precision.HIGHEST
    )
    total = tail[0:3] - landed[0:3, 0:ATOMS]
    for copy in returns:
        copy.wait_send()
    for copy in (2, 5, 6, 1, 0, 7, 4, 3):
        returns[copy].wait_recv()
        num = 7 - order[copy][0]
        both = dot(jnp.concatenate(split(back_in[num]), axis=0), sel[num])
        total = total + both[0:3] + both[8:11]
    out_ref[...] = jnp.concatenate([total, tail[3:4]], axis=0)


def hand_over(both, en_ref, fo_ref):
    en_ref[...] = both[3:4]
    for axis in range(3):
        fo_ref[axis] = both[axis : axis + 1]


def shards(
    features,
    displacement,
    neighbours,
    neighbour_count,
    species,
    send_list,
    send_count,
    w_center,
    w_neighbour,
    w_radial,
    w_hidden,
    w_tensor,
    readout,
    species_scale,
    species_shift,
):
    vmem = pl.BlockSpec(memory_space=pltpu.VMEM)
    hbm = pl.BlockSpec(memory_space=pl.ANY)
    both = pl.pallas_call(
        kernel,
        out_shape=jax.ShapeDtypeStruct((4, ATOMS), F32),
        in_specs=[vmem] * 7 + [hbm, hbm, vmem, hbm, hbm] + [vmem] * 3,
        out_specs=vmem,
        scratch_shapes=[
            pltpu.VMEM((WIDTH, HID), BF16),
            pltpu.VMEM((WIDTH, HID), BF16),
            pltpu.VMEM((HID, HID), BF16),
            pltpu.VMEM((HID, WIDTH), BF16),
            pltpu.VMEM((HID, WIDTH), BF16),
            pltpu.VMEM((HID, 128), BF16),
            pltpu.VMEM((HID, HID), BF16),
            pltpu.VMEM((CH, HID), BF16),
            pltpu.VMEM((8, GHOSTS, ATOMS), BF16),
            pltpu.VMEM((8, GHOSTS, WIDTH), BF16),
            pltpu.VMEM((8, GHOSTS, WIDTH), BF16),
            pltpu.VMEM((64, 128), F32),
            pltpu.VMEM((4, SLOTS, ATOMS), F32),
            pltpu.VMEM((7, SLOTS, ATOMS), F32),
            pltpu.VMEM((ATOMS + 8 * GHOSTS, EDGES), BF16),
            pltpu.VMEM((SLOTS, HID, ATOMS), F32),
            pltpu.VMEM((SLOTS, HID, ATOMS), F32),
            pltpu.VMEM((WIDTH, EDGES), BF16),
            pltpu.VMEM((HID, 2 * ATOMS), BF16),
            pltpu.VMEM((HID, 2 * ATOMS), BF16),
            pltpu.VMEM((SLOTS, CH, 2 * ATOMS), F32),
            pltpu.VMEM((8, 8, GHOSTS), F32),
            pltpu.VMEM((8, 8, GHOSTS), F32),
            pltpu.SemaphoreType.DMA((4,)),
            pltpu.SemaphoreType.DMA((8,)),
            pltpu.SemaphoreType.DMA((8,)),
            pltpu.SemaphoreType.DMA((8,)),
            pltpu.SemaphoreType.DMA((8,)),
        ],
        compiler_params=pltpu.CompilerParams(
            collective_id=0, has_side_effects=True, vmem_limit_bytes=56 * 1024 * 1024
        ),
        cost_estimate=pl.CostEstimate(
            flops=14_000_000_000, bytes_accessed=4_000_000, transcendentals=4_000_000
        ),
    )(
        features[0, 0],
        displacement.reshape(3, 1, EDGES),
        neighbours[0],
        neighbour_count[0],
        species[0],
        send_list[0, 0],
        send_count[0],
        w_center,
        w_neighbour,
        w_radial,
        w_hidden,
        w_tensor.T,
        readout[None],
        species_scale[None],
        species_shift[None],
    )
    energy, forces = pl.pallas_call(
        hand_over,
        out_shape=(
            jax.ShapeDtypeStruct((1, ATOMS), F32),
            jax.ShapeDtypeStruct((3, 1, ATOMS), F32),
        ),
        in_specs=[vmem],
        out_specs=(vmem, vmem),
    )(both)
    return energy[None], forces.reshape(1, 1, 3, ATOMS)


def solution(mesh):
    placed = (
        P("gx", "gy", None, None),
        P("gx", "gy", None, None),
        P("gx", "gy", None),
        P("gx", "gy", None),
        P("gx", "gy", None),
        P("gx", "gy", None, None),
        P("gx", "gy", None),
        P(),
        P(),
        P(),
        P(),
        P(),
        P(),
        P(),
        P(),
    )
    return jax.shard_map(
        shards,
        mesh=mesh,
        in_specs=placed,
        out_specs=(P("gx", "gy", None), P("gx", "gy", None, None)),
        check_vma=False,
    )
```

```python
import jax
import jax.numpy as jnp
from jax import lax
from jax.experimental import pallas as pl
from jax.experimental.pallas import tpu as pltpu
from jax.sharding import PartitionSpec as P

DIRECTIONS = ((-1, -1), (-1, 0), (-1, 1), (0, -1), (0, 1), (1, -1), (1, 0), (1, 1))
ATOMS = 256
SLOTS = 8
EDGES = ATOMS * SLOTS
GHOSTS = 192
WIDTH = 256
HID = 1024
CH = 64
F32 = jnp.float32
BF16 = jnp.bfloat16
MESH = pl.DeviceIdType.MESH


def iota(shape, dim):
    return lax.broadcasted_iota(jnp.int32, shape, dim)


def one_hot(hit):
    return jnp.where(hit, 1.0, 0.0).astype(BF16)


def dot(a, b):
    return jnp.dot(a, b, preferred_element_type=F32)


def silu_pair(value):
    gate = 0.5 * jnp.tanh(0.5 * value) + 0.5
    act = value * gate
    return act, gate + act * (1.0 - gate)


def split(value):
    high = value.astype(BF16)
    return high, (value - high.astype(F32)).astype(BF16)


def kernel(
    feat_hbm,
    disp_hbm,
    nbr_hbm,
    cnt_hbm,
    spc_hbm,
    lists_hbm,
    scnt_hbm,
    wc_hbm,
    wn_hbm,
    wr_hbm,
    wh_hbm,
    wtt_hbm,
    ro_hbm,
    sscale_hbm,
    sshift_hbm,
    out_ref,
    feat,
    disp,
    nbr,
    cnt,
    spc,
    lists,
    scnt,
    wr,
    ro,
    sscale,
    sshift,
    wc,
    wn,
    wh,
    wct,
    wnt,
    wrt,
    wht,
    wtt,
    sel,
    outg,
    ghost,
    stage,
    dsp,
    geo,
    oh,
    low_hot,
    high_hot,
    pre,
    drad,
    rows,
    act1,
    act2,
    tws,
    back_out,
    back_in,
    load_sem,
    send_sem,
    recv_sem,
    bsend_sem,
    brecv_sem,
):
    px, qy = lax.axis_index("gx"), lax.axis_index("gy")
    nx, ny = lax.axis_size("gx"), lax.axis_size("gy")

    def peer(ox, oy):
        return lax.rem(px + (ox + nx), nx), lax.rem(qy + (oy + ny), ny)

    core = lax.rem(qy, 2)
    side = 2 * core - 1
    order = [
        (6 + side, peer(1, side)),
        (1 + side, peer(-1, side)),
        (3 + core, peer(0, side)),
        (6 - side, peer(1, -side)),
        (1 - side, peer(-1, -side)),
        (6, peer(1, 0)),
        (1, peer(-1, 0)),
        (4 - core, peer(0, -side)),
    ]
    barrier = pltpu.get_barrier_semaphore()
    for _, device in order:
        pl.semaphore_signal(barrier, inc=1, device_id=device, device_id_type=MESH)

    pairs = (
        (lists_hbm, lists),
        (scnt_hbm, scnt),
        (feat_hbm, feat),
        (disp_hbm, disp),
        (nbr_hbm, nbr),
        (cnt_hbm, cnt),
        (spc_hbm, spc),
        (sscale_hbm, sscale),
        (sshift_hbm, sshift),
        (ro_hbm, ro),
        (wr_hbm, wr),
        (wc_hbm, wc),
        (wn_hbm, wn),
        (wh_hbm, wh),
        (wtt_hbm, wtt),
    )
    loads = [
        pltpu.make_async_copy(src, dst, load_sem.at[num]) for num, (src, dst) in enumerate(pairs)
    ]
    for load in loads:
        load.start()
    for load in loads[0:3]:
        load.wait()

    ids = jnp.concatenate([lists[...].astype(F32), jnp.zeros((8, ATOMS - GHOSTS), F32)], axis=1)
    slot = iota((ATOMS, 8), 0)
    kept = jnp.where((slot < scnt[...]) & (slot < GHOSTS), jnp.transpose(ids), -1.0)
    lane = iota((ATOMS, ATOMS), 1).astype(F32)
    for num in range(8):
        hit = one_hot(kept[:, num : num + 1] == lane)
        for half in range(2):
            sel[num * 128 : (num + 1) * 128, half * 256 : (half + 1) * 256] = hit[
                half * 128 : (half + 1) * 128
            ]
        outg[num] = dot(hit[0:GHOSTS], feat[...]).astype(BF16)
    pl.semaphore_wait(barrier, 8)
    sends = []
    for num, peer in order:
        copy = pltpu.make_async_remote_copy(
            src_ref=outg.at[num],
            dst_ref=ghost.at[7 - num],
            send_sem=send_sem.at[num],
            recv_sem=recv_sem.at[7 - num],
            device_id=peer,
            device_id_type=MESH,
        )
        copy.start()
        sends.append(copy)

    for load in loads[3:11]:
        load.wait()

    for axis in range(3):
        for c in range(16):
            stage[pl.ds(axis * 16 + c, 1), :] = disp[axis, :, c * 128 : (c + 1) * 128]
    for c in range(16):
        stage[pl.ds(48 + c, 1), :] = nbr[0:1, c * 128 : (c + 1) * 128].astype(F32)
    turned = jnp.transpose(stage[...])
    for row in range(4):
        for a in range(16):
            dsp[row, :, a * 16 : (a + 1) * 16] = turned[
                a * 8 : (a + 1) * 8, row * 16 : (row + 1) * 16
            ]
    col = iota((ATOMS, ATOMS), 1)
    swap = iota((ATOMS, ATOMS), 0) == (col & 15) * 16 + (col >> 4)
    swap_b = one_hot(swap)
    small = jnp.concatenate(
        [cnt[...].astype(F32), spc[...].astype(F32), jnp.zeros((14, ATOMS), F32)], axis=0
    ).astype(BF16)
    small = dot(small, swap_b)
    count, kind = small[0:1], small[1:2]
    scale = jnp.zeros((1, ATOMS), F32)
    shift = jnp.zeros((1, ATOMS), F32)
    for num in range(4):
        hit = kind == float(num)
        scale = jnp.where(hit, sscale[0:1, num : num + 1], scale)
        shift = jnp.where(hit, sshift[0:1, num : num + 1], shift)
    squared = dsp[0] * dsp[0] + dsp[1] * dsp[1] + dsp[2] * dsp[2]
    distance = jnp.sqrt(squared)
    inverse = 1.0 / distance
    live = jnp.where(iota((SLOTS, ATOMS), 0).astype(F32) < count, 1.0, 0.0)
    for axis in range(3):
        geo[axis] = dsp[axis] * inverse
    geo[3] = jnp.square(1.0 - squared) * live
    geo[4] = distance
    geo[5] = -4.0 * (1.0 - squared) * live
    geo[6] = inverse

    wrt[...] = jnp.transpose(
        jnp.concatenate([wr[...].astype(F32), jnp.zeros((120, HID), F32)], axis=0)
    ).astype(BF16)
    loads[11].wait()
    for num in range(4):
        wct[num * 256 : (num + 1) * 256, :] = jnp.transpose(wc[:, num * 256 : (num + 1) * 256])
    loads[12].wait()
    for num in range(4):
        wnt[num * 256 : (num + 1) * 256, :] = jnp.transpose(wn[:, num * 256 : (num + 1) * 256])
    loads[13].wait()

    def turn(num, carry):
        start = pl.multiple_of(num * 256, 256)
        for part in range(4):
            wht[pl.ds(start, 256), part * 256 : (part + 1) * 256] = jnp.transpose(
                wh[part * 256 : (part + 1) * 256, pl.ds(start, 256)]
            )
        return carry

    lax.fori_loop(0, 4, turn, 0)
    loads[14].wait()

    feat_t = jnp.transpose(feat[...])
    feat_p = dot(feat_t, swap_b).astype(BF16)
    unit_id = iota((16, ATOMS), 0)
    centre_at = (unit_id.astype(F32) + 1.0) * 0.125
    row_id = iota((256, ATOMS), 0).astype(F32)

    def before(k, carry):
        lanes = pl.ds(pl.multiple_of(k * 256, 256), 256)
        ids = dsp[3, pl.ds(k, 1), :]
        for part in range(7):
            oh[part * 256 : (part + 1) * 256, lanes] = one_hot(row_id + (part * 256.0) == ids)
        rows[:, lanes] = dot(feat_t, oh[0:256, lanes]).astype(BF16)
        own = ids < float(ATOMS)
        block = jnp.zeros((1, ATOMS), F32)
        for num in range(1, 8):
            block = block + jnp.where(ids >= float(ATOMS + num * GHOSTS), 1.0, 0.0)
        inside = jnp.where(own, ids, ids - float(ATOMS) - block * float(GHOSTS))
        upper = jnp.where(inside >= 128.0, 1.0, 0.0)
        low_hot[:, lanes] = one_hot(row_id[0:128] == inside - 128.0 * upper)
        part_id = jnp.where(own, 16.0, 2.0 * block) + upper
        high_hot[:, lanes] = one_hot(row_id[0:32] == part_id)
        offset = (geo[4, pl.ds(k, 1), :] - centre_at) * 4.0
        basis = jnp.where(unit_id < 8, jnp.exp(-offset * offset), 0.0)
        both = jnp.concatenate([basis, -8.0 * offset * basis], axis=1).astype(BF16)
        both = jnp.concatenate([both, jnp.zeros((112, 512), BF16)], axis=0)
        for part in range(4):
            here = slice(part * 256, (part + 1) * 256)
            radial = dot(wrt[here, :], both)
            pre[k, here, :] = radial[:, :256] + dot(wct[here, :], feat_p)
            drad[k, here, :] = radial[:, 256:]
        return carry

    lax.fori_loop(0, SLOTS, before, 0)

    def take(num):
        turned = jnp.transpose(ghost[num])
        first = pl.multiple_of(ATOMS + num * GHOSTS, 64)
        for part in range(4):
            here = slice(part * 512, (part + 1) * 512)
            found = dot(turned, oh[pl.ds(first, GHOSTS), here])
            rows[:, here] = rows[:, here] + found.astype(BF16)

    for copy in sends:
        copy.wait_send()
    for copy in (2, 5, 6, 1, 0, 7, 4, 3):
        sends[copy].wait_recv()
        take(7 - order[copy][0])

    def first(k, at):
        found = rows[:, k * 256 : (k + 1) * 256]
        for part in range(4):
            here = slice(part * 256, (part + 1) * 256)
            act, slope = silu_pair(dot(wnt[here, :], found) + pre[k, here, :])
            act1[here, at : at + 256] = act.astype(BF16)
            act1[here, at + 256 : at + 512] = (slope * drad[k, here, :]).astype(BF16)

    def second(at):
        for part in range(4):
            here = slice(part * 256, (part + 1) * 256)
            hidden = dot(wht[here, :], act1[:, at : at + 512])
            act, slope = silu_pair(hidden[:, :256])
            act2[here, at : at + 256] = act.astype(BF16)
            act2[here, at + 256 : at + 512] = (slope * hidden[:, 256:]).astype(BF16)

    def product(k, weight, sums):
        tws[k] = weight
        unit = [geo[axis, k : k + 1, :] for axis in range(3)]
        row = rows[:, k * 256 : (k + 1) * 256].astype(F32)
        s, v = row[0:CH], [row[CH * (m + 1) : CH * (m + 2)] for m in range(3)]
        w = weight[:, :256] * geo[3, k : k + 1, :]
        out = [sums[0] + w * (s + unit[0] * v[0] + unit[1] * v[1] + unit[2] * v[2])]
        for m in range(3):
            out.append(sums[m + 1] + w * (s * unit[m] + v[m]))
        return tuple(out)

    sums = tuple(jnp.zeros((CH, ATOMS), F32) for _ in range(4))
    for k in range(0, SLOTS, 2):
        first(k, 0)
        first(k + 1, 512)
        second(0)
        second(512)
        weight = dot(wtt[...], act2[...])
        sums = product(k, weight[:, 0:512], sums)
        sums = product(k + 1, weight[:, 512:], sums)

    eye = iota((CH, CH), 0) == iota((CH, CH), 1)
    read = jnp.sum(jnp.where(eye, ro[...], 0.0), axis=1, keepdims=True)
    inv = sums[0] * sums[0] + sums[1] * sums[1] + sums[2] * sums[2] + sums[3] * sums[3]
    energy = scale * jnp.sum(inv * read, axis=0, keepdims=True) + shift
    factor = 2.0 * scale * read
    cot = [factor * total for total in sums]

    def slopes(k, own, landed):
        lanes = slice(k * 256, (k + 1) * 256)
        unit = [geo[axis, pl.ds(k, 1), :] for axis in range(3)]
        env = geo[3, pl.ds(k, 1), :]
        row = rows[:, lanes].astype(F32)
        s, v = row[0:CH], [row[CH * (m + 1) : CH * (m + 2)] for m in range(3)]
        weight = tws[k]
        tw, dtw = weight[:, :256], weight[:, 256:]
        q = cot[0] * (s + unit[0] * v[0] + unit[1] * v[1] + unit[2] * v[2])
        for m in range(3):
            q = q + cot[m + 1] * (s * unit[m] + v[m])
        by_dist = env * jnp.sum(q * dtw, axis=0, keepdims=True)
        by_env = jnp.sum(q * tw, axis=0, keepdims=True)
        w = tw * env
        by_unit = [
            jnp.sum(w * (cot[0] * v[m] + cot[m + 1] * s), axis=0, keepdims=True) for m in range(3)
        ]
        along = by_unit[0] * unit[0] + by_unit[1] * unit[1] + by_unit[2] * unit[2]
        inverse_k = geo[6, pl.ds(k, 1), :]
        common = by_dist - along * inverse_k
        scaled = by_env * geo[5, pl.ds(k, 1), :]
        grad = jnp.concatenate(
            [
                common * unit[m] + scaled * dsp[m, pl.ds(k, 1), :] + by_unit[m] * inverse_k
                for m in range(3)
            ]
            + [jnp.zeros((5, ATOMS), F32)],
            axis=0,
        )
        high, low = split(grad[0:3])
        flat = jnp.concatenate([high, low], axis=0)
        spread = lax.dot_general(
            jnp.concatenate([high_hot[:, lanes] * flat[m : m + 1] for m in range(6)], axis=0),
            low_hot[:, lanes],
            (((1,), (1,)), ((), ())),
            preferred_element_type=F32,
        )
        return own + grad, landed + spread

    own = jnp.zeros((8, ATOMS), F32)
    landed = jnp.zeros((192, 128), F32)
    for k in range(SLOTS):
        own, landed = slopes(k, own, landed)
    landed = landed[0:96] + landed[96:192]
    for num in range(8):
        pair = [landed[m * 32 + 2 * num : m * 32 + 2 * num + 2] for m in range(3)]
        none = jnp.zeros((1, 128), F32)
        back_out[num] = jnp.concatenate(
            [side_row for half in range(2) for side_row in [p[half : half + 1] for p in pair] + [none]],
            axis=0,
        )
    returns = []
    for num, device in order:
        copy = pltpu.make_async_remote_copy(
            src_ref=back_out.at[num],
            dst_ref=back_in.at[7 - num],
            send_sem=bsend_sem.at[num],
            recv_sem=brecv_sem.at[7 - num],
            device_id=device,
            device_id_type=MESH,
        )
        copy.start()
        returns.append(copy)
    tail = jnp.concatenate([own[0:3], energy, jnp.zeros((4, ATOMS), F32)], axis=0)
    tail = jnp.dot(
        tail, jnp.where(swap, 1.0, 0.0), preferred_element_type=F32, precision=lax.Precision.HIGHEST
    )
    total = tail[0:3] - jnp.concatenate(
        [
            jnp.concatenate([landed[m * 32 + 16 + half : m * 32 + 17 + half] for m in range(3)], axis=0)
            for half in range(2)
        ],
        axis=1,
    )
    for copy in returns:
        copy.wait_recv()
    back = jnp.concatenate([back_in[num] for num in range(8)], axis=1)
    both = dot(jnp.concatenate(split(back), axis=0), sel[...])
    both = both[0:8] + both[8:16]
    total = total + both[0:3, 0:ATOMS] + both[4:7, ATOMS:]
    for copy in returns:
        copy.wait_send()
    for axis in range(3):
        out_ref[axis] = total[axis : axis + 1]
    out_ref[3] = tail[3:4]


def hand_over(both, en_ref, fo_ref, sem):
    energy = pltpu.make_async_copy(both.at[3], en_ref, sem.at[0])
    forces = pltpu.make_async_copy(both.at[pl.ds(0, 3)], fo_ref, sem.at[1])
    energy.start()
    forces.start()
    energy.wait()
    forces.wait()


def shards(
    features,
    displacement,
    neighbours,
    neighbour_count,
    species,
    send_list,
    send_count,
    w_center,
    w_neighbour,
    w_radial,
    w_hidden,
    w_tensor,
    readout,
    species_scale,
    species_shift,
):
    vmem = pl.BlockSpec(memory_space=pltpu.VMEM)
    hbm = pl.BlockSpec(memory_space=pl.ANY)
    both = pl.pallas_call(
        kernel,
        out_shape=jax.ShapeDtypeStruct((4, 1, ATOMS), F32),
        in_specs=[hbm] * 15,
        out_specs=vmem,
        scratch_shapes=[
            pltpu.VMEM((ATOMS, WIDTH), BF16),
            pltpu.VMEM((3, 1, EDGES), F32),
            pltpu.VMEM((1, EDGES), jnp.int32),
            pltpu.VMEM((1, ATOMS), jnp.int32),
            pltpu.VMEM((1, ATOMS), jnp.int32),
            pltpu.VMEM((8, GHOSTS), jnp.int32),
            pltpu.VMEM((1, 8), jnp.int32),
            pltpu.VMEM((8, HID), BF16),
            pltpu.VMEM((1, CH), F32),
            pltpu.VMEM((1, 4), F32),
            pltpu.VMEM((1, 4), F32),
            pltpu.VMEM((WIDTH, HID), BF16),
            pltpu.VMEM((WIDTH, HID), BF16),
            pltpu.VMEM((HID, HID), BF16),
            pltpu.VMEM((HID, WIDTH), BF16),
            pltpu.VMEM((HID, WIDTH), BF16),
            pltpu.VMEM((HID, 128), BF16),
            pltpu.VMEM((HID, HID), BF16),
            pltpu.VMEM((CH, HID), BF16),
            pltpu.VMEM((8 * 128, 2 * ATOMS), BF16),
            pltpu.VMEM((8, GHOSTS, WIDTH), BF16),
            pltpu.VMEM((8, GHOSTS, WIDTH), BF16),
            pltpu.VMEM((64, 128), F32),
            pltpu.VMEM((4, SLOTS, ATOMS), F32),
            pltpu.VMEM((7, SLOTS, ATOMS), F32),
            pltpu.VMEM((ATOMS + 8 * GHOSTS, EDGES), BF16),
            pltpu.VMEM((128, EDGES), BF16),
            pltpu.VMEM((32, EDGES), BF16),
            pltpu.VMEM((SLOTS, HID, ATOMS), F32),
            pltpu.VMEM((SLOTS, HID, ATOMS), F32),
            pltpu.VMEM((WIDTH, EDGES), BF16),
            pltpu.VMEM((HID, 4 * ATOMS), BF16),
            pltpu.VMEM((HID, 4 * ATOMS), BF16),
            pltpu.VMEM((SLOTS, CH, 2 * ATOMS), F32),
            pltpu.VMEM((8, 8, 128), F32),
            pltpu.VMEM((8, 8, 128), F32),
            pltpu.SemaphoreType.DMA((15,)),
            pltpu.SemaphoreType.DMA((8,)),
            pltpu.SemaphoreType.DMA((8,)),
            pltpu.SemaphoreType.DMA((8,)),
            pltpu.SemaphoreType.DMA((8,)),
        ],
        compiler_params=pltpu.CompilerParams(
            collective_id=0, has_side_effects=True, vmem_limit_bytes=56 * 1024 * 1024
        ),
        cost_estimate=pl.CostEstimate(
            flops=14_000_000_000, bytes_accessed=4_000_000, transcendentals=4_000_000
        ),
    )(
        features[0, 0],
        displacement.reshape(3, 1, EDGES),
        neighbours[0],
        neighbour_count[0],
        species[0],
        send_list[0, 0],
        send_count[0],
        w_center,
        w_neighbour,
        w_radial,
        w_hidden,
        w_tensor.T,
        readout[None],
        species_scale[None],
        species_shift[None],
    )
    energy, forces = pl.pallas_call(
        hand_over,
        out_shape=(
            jax.ShapeDtypeStruct((1, ATOMS), F32),
            jax.ShapeDtypeStruct((3, 1, ATOMS), F32),
        ),
        in_specs=[hbm],
        out_specs=(hbm, hbm),
        scratch_shapes=[pltpu.SemaphoreType.DMA((2,))],
    )(both)
    return energy[None], forces.reshape(1, 1, 3, ATOMS)


def solution(mesh):
    placed = (
        P("gx", "gy", None, None),
        P("gx", "gy", None, None),
        P("gx", "gy", None),
        P("gx", "gy", None),
        P("gx", "gy", None),
        P("gx", "gy", None, None),
        P("gx", "gy", None),
        P(),
        P(),
        P(),
        P(),
        P(),
        P(),
        P(),
        P(),
    )
    return jax.shard_map(
        shards,
        mesh=mesh,
        in_specs=placed,
        out_specs=(P("gx", "gy", None), P("gx", "gy", None, None)),
        check_vma=False,
    )
```

```python
import jax
import jax.numpy as jnp
from jax import lax
from jax.experimental import pallas as pl
from jax.experimental.pallas import tpu as pltpu
from jax.sharding import PartitionSpec as P

DIRECTIONS = ((-1, -1), (-1, 0), (-1, 1), (0, -1), (0, 1), (1, -1), (1, 0), (1, 1))
ATOMS = 256
SLOTS = 8
EDGES = ATOMS * SLOTS
GHOSTS = 192
WIDTH = 256
HID = 1024
CH = 64
F32 = jnp.float32
BF16 = jnp.bfloat16
MESH = pl.DeviceIdType.MESH


def iota(shape, dim):
    return lax.broadcasted_iota(jnp.int32, shape, dim)


def one_hot(hit):
    return jnp.where(hit, 1.0, 0.0).astype(BF16)


def dot(a, b):
    return jnp.dot(a, b, preferred_element_type=F32)


def silu_pair(value):
    gate = 0.5 * jnp.tanh(0.5 * value) + 0.5
    act = value * gate
    return act, gate + act * (1.0 - gate)


def split(value):
    high = value.astype(BF16)
    return high, (value - high.astype(F32)).astype(BF16)


def kernel(
    feat_hbm,
    disp_hbm,
    nbr_hbm,
    cnt_hbm,
    spc_hbm,
    lists_hbm,
    scnt_hbm,
    wc_hbm,
    wn_hbm,
    wr_hbm,
    wh_hbm,
    wtt_hbm,
    ro_hbm,
    sscale_hbm,
    sshift_hbm,
    out_ref,
    feat,
    disp,
    nbr,
    cnt,
    spc,
    lists,
    scnt,
    wr,
    ro,
    sscale,
    sshift,
    wc,
    wn,
    wh,
    wct,
    wnt,
    wrt,
    wht,
    wtt,
    sel,
    outg,
    ghost,
    stage,
    dsp,
    geo,
    oh,
    low_hot,
    high_hot,
    pre,
    drad,
    rows,
    act1,
    act2,
    tws,
    back_out,
    back_in,
    load_sem,
    send_sem,
    recv_sem,
    bsend_sem,
    brecv_sem,
):
    px, qy = lax.axis_index("gx"), lax.axis_index("gy")
    nx, ny = lax.axis_size("gx"), lax.axis_size("gy")

    def peer(ox, oy):
        return lax.rem(px + (ox + nx), nx), lax.rem(qy + (oy + ny), ny)

    core = lax.rem(qy, 2)
    side = 2 * core - 1
    order = [
        (4 - core, peer(0, -side), 0),
        (6 + side, peer(1, side), 1),
        (1 + side, peer(-1, side), 2),
        (3 + core, peer(0, side), 3),
        (6 - side, peer(1, -side), 4),
        (1 - side, peer(-1, -side), 5),
        (6, peer(1, 0), 6),
        (1, peer(-1, 0), 7),
    ]
    origin = [
        (4 - core, peer(0, -side)),
        (1 + side, peer(-1, side)),
        (6 + side, peer(1, side)),
        (3 + core, peer(0, side)),
        (1 - side, peer(-1, -side)),
        (6 - side, peer(1, -side)),
        (1, peer(-1, 0)),
        (6, peer(1, 0)),
    ]
    base = [(ATOMS + GHOSTS * block + jnp.int32(0)).astype(F32) for block, _ in origin]
    barrier = pltpu.get_barrier_semaphore()
    for _, device, _ in order:
        pl.semaphore_signal(barrier, inc=1, device_id=device, device_id_type=MESH)

    pairs = (
        (lists_hbm, lists),
        (scnt_hbm, scnt),
        (feat_hbm, feat),
        (disp_hbm, disp),
        (nbr_hbm, nbr),
        (cnt_hbm, cnt),
        (spc_hbm, spc),
        (sscale_hbm, sscale),
        (sshift_hbm, sshift),
        (ro_hbm, ro),
        (wr_hbm, wr),
        (wc_hbm, wc),
        (wn_hbm, wn),
        (wh_hbm, wh),
        (wtt_hbm, wtt),
    )
    loads = [
        pltpu.make_async_copy(src, dst, load_sem.at[num]) for num, (src, dst) in enumerate(pairs)
    ]
    for load in loads:
        load.start()
    for load in loads[0:3]:
        load.wait()

    ids = jnp.concatenate([lists[...].astype(F32), jnp.zeros((8, ATOMS - GHOSTS), F32)], axis=1)
    slot = iota((ATOMS, 8), 0)
    kept = jnp.where((slot < scnt[...]) & (slot < GHOSTS), jnp.transpose(ids), -1.0)
    lane = iota((ATOMS, ATOMS), 1).astype(F32)
    for num in range(8):
        hit = one_hot(kept[:, num : num + 1] == lane)
        for half in range(2):
            sel[num * 128 : (num + 1) * 128, half * 256 : (half + 1) * 256] = hit[
                half * 128 : (half + 1) * 128
            ]
        outg[num] = dot(hit[0:GHOSTS], feat[...]).astype(BF16)
    pl.semaphore_wait(barrier, 8)
    sends = []
    for num, device, place in order:
        copy = pltpu.make_async_remote_copy(
            src_ref=outg.at[num],
            dst_ref=ghost.at[place],
            send_sem=send_sem.at[place],
            recv_sem=recv_sem.at[place],
            device_id=device,
            device_id_type=MESH,
        )
        copy.start()
        sends.append(copy)

    for load in loads[3:11]:
        load.wait()

    for axis in range(3):
        for c in range(16):
            stage[pl.ds(axis * 16 + c, 1), :] = disp[axis, :, c * 128 : (c + 1) * 128]
    for c in range(16):
        stage[pl.ds(48 + c, 1), :] = nbr[0:1, c * 128 : (c + 1) * 128].astype(F32)
    turned = jnp.transpose(stage[...])
    for row in range(4):
        for a in range(16):
            dsp[row, :, a * 16 : (a + 1) * 16] = turned[
                a * 8 : (a + 1) * 8, row * 16 : (row + 1) * 16
            ]
    col = iota((ATOMS, ATOMS), 1)
    swap = iota((ATOMS, ATOMS), 0) == (col & 15) * 16 + (col >> 4)
    swap_b = one_hot(swap)
    small = jnp.concatenate(
        [cnt[...].astype(F32), spc[...].astype(F32), jnp.zeros((14, ATOMS), F32)], axis=0
    ).astype(BF16)
    small = dot(small, swap_b)
    count, kind = small[0:1], small[1:2]
    scale = jnp.zeros((1, ATOMS), F32)
    shift = jnp.zeros((1, ATOMS), F32)
    for num in range(4):
        hit = kind == float(num)
        scale = jnp.where(hit, sscale[0:1, num : num + 1], scale)
        shift = jnp.where(hit, sshift[0:1, num : num + 1], shift)
    squared = dsp[0] * dsp[0] + dsp[1] * dsp[1] + dsp[2] * dsp[2]
    distance = jnp.sqrt(squared)
    inverse = 1.0 / distance
    live = jnp.where(iota((SLOTS, ATOMS), 0).astype(F32) < count, 1.0, 0.0)
    for axis in range(3):
        geo[axis] = dsp[axis] * inverse
    geo[3] = jnp.square(1.0 - squared) * live
    geo[4] = distance
    geo[5] = -4.0 * (1.0 - squared) * live
    geo[6] = inverse

    wrt[...] = jnp.transpose(
        jnp.concatenate([wr[...].astype(F32), jnp.zeros((120, HID), F32)], axis=0)
    ).astype(BF16)
    loads[11].wait()
    for num in range(4):
        wct[num * 256 : (num + 1) * 256, :] = jnp.transpose(wc[:, num * 256 : (num + 1) * 256])
    loads[12].wait()
    for num in range(4):
        wnt[num * 256 : (num + 1) * 256, :] = jnp.transpose(wn[:, num * 256 : (num + 1) * 256])
    loads[13].wait()

    def turn(num, carry):
        start = pl.multiple_of(num * 256, 256)
        for part in range(4):
            wht[pl.ds(start, 256), part * 256 : (part + 1) * 256] = jnp.transpose(
                wh[part * 256 : (part + 1) * 256, pl.ds(start, 256)]
            )
        return carry

    lax.fori_loop(0, 4, turn, 0)
    loads[14].wait()

    feat_t = jnp.transpose(feat[...])
    feat_p = dot(feat_t, swap_b).astype(BF16)
    unit_id = iota((16, ATOMS), 0)
    centre_at = (unit_id.astype(F32) + 1.0) * 0.125
    row_id = iota((256, ATOMS), 0).astype(F32)

    def before(k, carry):
        lanes = pl.ds(pl.multiple_of(k * 256, 256), 256)
        ids = dsp[3, pl.ds(k, 1), :]
        oh[0:ATOMS, lanes] = one_hot(row_id == ids)
        inside = ids
        place = jnp.full((1, ATOMS), 16.0, F32)
        for num in range(8):
            start = ATOMS + num * GHOSTS
            away = ids - base[num]
            oh[start : start + GHOSTS, lanes] = one_hot(row_id[0:GHOSTS] == away)
            hit = (away >= 0.0) & (away < float(GHOSTS))
            inside = jnp.where(hit, away, inside)
            place = jnp.where(hit, 2.0 * num, place)
        rows[:, lanes] = dot(feat_t, oh[0:256, lanes]).astype(BF16)
        upper = jnp.where(inside >= 128.0, 1.0, 0.0)
        low_hot[:, lanes] = one_hot(row_id[0:128] == inside - 128.0 * upper)
        high_hot[:, lanes] = one_hot(row_id[0:32] == place + upper)
        offset = (geo[4, pl.ds(k, 1), :] - centre_at) * 4.0
        basis = jnp.where(unit_id < 8, jnp.exp(-offset * offset), 0.0)
        both = jnp.concatenate([basis, -8.0 * offset * basis], axis=1).astype(BF16)
        both = jnp.concatenate([both, jnp.zeros((112, 512), BF16)], axis=0)
        for part in range(4):
            here = slice(part * 256, (part + 1) * 256)
            radial = dot(wrt[here, :], both)
            pre[k, here, :] = radial[:, :256] + dot(wct[here, :], feat_p)
            drad[k, here, :] = radial[:, 256:]
        return carry

    lax.fori_loop(0, SLOTS, before, 0)

    def landed_rows(start, stop):
        for num in range(start, stop):
            sends[num].wait_recv()
        return jnp.transpose(
            jnp.concatenate([ghost[num] for num in range(start, stop)], axis=0)
        )

    for start, stop in ((0, 1), (1, 4), (4, 8)):
        turned = landed_rows(start, stop)
        ids = slice(ATOMS + start * GHOSTS, ATOMS + stop * GHOSTS)
        for part in range(4):
            here = slice(part * 512, (part + 1) * 512)
            rows[:, here] = rows[:, here] + dot(turned, oh[ids, here]).astype(BF16)
    for copy in sends:
        copy.wait_send()

    def first(k, at):
        lanes = slice(k * 256, (k + 1) * 256)
        found = rows[:, lanes]
        for part in range(4):
            here = slice(part * 256, (part + 1) * 256)
            act, slope = silu_pair(dot(wnt[here, :], found) + pre[k, here, :])
            act1[here, at : at + 256] = act.astype(BF16)
            act1[here, at + 256 : at + 512] = (slope * drad[k, here, :]).astype(BF16)

    def second(at):
        for part in range(4):
            here = slice(part * 256, (part + 1) * 256)
            hidden = dot(wht[here, :], act1[:, at : at + 512])
            act, slope = silu_pair(hidden[:, :256])
            act2[here, at : at + 256] = act.astype(BF16)
            act2[here, at + 256 : at + 512] = (slope * hidden[:, 256:]).astype(BF16)

    def product(k, weight, sums):
        unit = [geo[axis, k : k + 1, :] for axis in range(3)]
        row = rows[:, k * 256 : (k + 1) * 256].astype(F32)
        s, v = row[0:CH], [row[CH * (m + 1) : CH * (m + 2)] for m in range(3)]
        w = weight[:, :256] * geo[3, k : k + 1, :]
        out = [sums[0] + w * (s + unit[0] * v[0] + unit[1] * v[1] + unit[2] * v[2])]
        for m in range(3):
            out.append(sums[m + 1] + w * (s * unit[m] + v[m]))
        return tuple(out)

    sums = tuple(jnp.zeros((CH, ATOMS), F32) for _ in range(4))
    for k in range(0, SLOTS, 2):
        first(k, 0)
        first(k + 1, 512)
        second(0)
        second(512)
        tws[k // 2] = dot(wtt[...], act2[...])
    for k in range(SLOTS):
        sums = product(k, tws[k // 2, :, (k % 2) * 512 : (k % 2) * 512 + 512], sums)

    eye = iota((CH, CH), 0) == iota((CH, CH), 1)
    read = jnp.sum(jnp.where(eye, ro[...], 0.0), axis=1, keepdims=True)
    inv = sums[0] * sums[0] + sums[1] * sums[1] + sums[2] * sums[2] + sums[3] * sums[3]
    energy = scale * jnp.sum(inv * read, axis=0, keepdims=True) + shift
    factor = 2.0 * scale * read
    cot = [factor * total for total in sums]

    def slopes(k, own, landed):
        lanes = slice(k * 256, (k + 1) * 256)
        unit = [geo[axis, pl.ds(k, 1), :] for axis in range(3)]
        env = geo[3, pl.ds(k, 1), :]
        row = rows[:, lanes].astype(F32)
        s, v = row[0:CH], [row[CH * (m + 1) : CH * (m + 2)] for m in range(3)]
        weight = tws[k // 2, :, (k % 2) * 512 : (k % 2) * 512 + 512]
        tw, dtw = weight[:, :256], weight[:, 256:]
        q = cot[0] * (s + unit[0] * v[0] + unit[1] * v[1] + unit[2] * v[2])
        for m in range(3):
            q = q + cot[m + 1] * (s * unit[m] + v[m])
        by_dist = env * jnp.sum(q * dtw, axis=0, keepdims=True)
        by_env = jnp.sum(q * tw, axis=0, keepdims=True)
        w = tw * env
        by_unit = [
            jnp.sum(w * (cot[0] * v[m] + cot[m + 1] * s), axis=0, keepdims=True) for m in range(3)
        ]
        along = by_unit[0] * unit[0] + by_unit[1] * unit[1] + by_unit[2] * unit[2]
        inverse_k = geo[6, pl.ds(k, 1), :]
        common = by_dist - along * inverse_k
        scaled = by_env * geo[5, pl.ds(k, 1), :]
        grad = jnp.concatenate(
            [
                common * unit[m] + scaled * dsp[m, pl.ds(k, 1), :] + by_unit[m] * inverse_k
                for m in range(3)
            ]
            + [jnp.zeros((5, ATOMS), F32)],
            axis=0,
        )
        high, low = split(grad[0:3])
        flat = jnp.concatenate([high, low], axis=0)
        spread = lax.dot_general(
            jnp.concatenate([high_hot[:, lanes] * flat[m : m + 1] for m in range(6)], axis=0),
            low_hot[:, lanes],
            (((1,), (1,)), ((), ())),
            preferred_element_type=F32,
        )
        return own + grad, landed + spread

    own = jnp.zeros((8, ATOMS), F32)
    landed = jnp.zeros((192, 128), F32)
    for k in range(SLOTS):
        own, landed = slopes(k, own, landed)
    landed = landed[0:96] + landed[96:192]
    for num in range(8):
        pair = [landed[m * 32 + 2 * num : m * 32 + 2 * num + 2] for m in range(3)]
        none = jnp.zeros((1, 128), F32)
        back_out[num] = jnp.concatenate(
            [side_row for half in range(2) for side_row in [p[half : half + 1] for p in pair] + [none]],
            axis=0,
        )
    returns = []
    for place in (1, 2, 3, 4, 5, 6, 7, 0):
        block, device = origin[place]
        copy = pltpu.make_async_remote_copy(
            src_ref=back_out.at[place],
            dst_ref=back_in.at[7 - block],
            send_sem=bsend_sem.at[place],
            recv_sem=brecv_sem.at[7 - block],
            device_id=device,
            device_id_type=MESH,
        )
        copy.start()
        returns.append(copy)
    tail = jnp.concatenate([own[0:3], energy, jnp.zeros((4, ATOMS), F32)], axis=0)
    tail = jnp.dot(
        tail, jnp.where(swap, 1.0, 0.0), preferred_element_type=F32, precision=lax.Precision.HIGHEST
    )
    total = tail[0:3] - jnp.concatenate(
        [
            jnp.concatenate([landed[m * 32 + 16 + half : m * 32 + 17 + half] for m in range(3)], axis=0)
            for half in range(2)
        ],
        axis=1,
    )
    for copy in returns:
        copy.wait_recv()
    back = jnp.concatenate([back_in[num] for num in range(8)], axis=1)
    both = dot(jnp.concatenate(split(back), axis=0), sel[...])
    both = both[0:8] + both[8:16]
    total = total + both[0:3, 0:ATOMS] + both[4:7, ATOMS:]
    for copy in returns:
        copy.wait_send()
    for axis in range(3):
        out_ref[axis] = total[axis : axis + 1]
    out_ref[3] = tail[3:4]


def hand_over(both, en_ref, fo_ref, sem):
    energy = pltpu.make_async_copy(both.at[3], en_ref, sem.at[0])
    forces = pltpu.make_async_copy(both.at[pl.ds(0, 3)], fo_ref, sem.at[1])
    energy.start()
    forces.start()
    energy.wait()
    forces.wait()


def shards(
    features,
    displacement,
    neighbours,
    neighbour_count,
    species,
    send_list,
    send_count,
    w_center,
    w_neighbour,
    w_radial,
    w_hidden,
    w_tensor,
    readout,
    species_scale,
    species_shift,
):
    vmem = pl.BlockSpec(memory_space=pltpu.VMEM)
    hbm = pl.BlockSpec(memory_space=pl.ANY)
    both = pl.pallas_call(
        kernel,
        out_shape=jax.ShapeDtypeStruct((4, 1, ATOMS), F32),
        in_specs=[hbm] * 15,
        out_specs=vmem,
        scratch_shapes=[
            pltpu.VMEM((ATOMS, WIDTH), BF16),
            pltpu.VMEM((3, 1, EDGES), F32),
            pltpu.VMEM((1, EDGES), jnp.int32),
            pltpu.VMEM((1, ATOMS), jnp.int32),
            pltpu.VMEM((1, ATOMS), jnp.int32),
            pltpu.VMEM((8, GHOSTS), jnp.int32),
            pltpu.VMEM((1, 8), jnp.int32),
            pltpu.VMEM((8, HID), BF16),
            pltpu.VMEM((1, CH), F32),
            pltpu.VMEM((1, 4), F32),
            pltpu.VMEM((1, 4), F32),
            pltpu.VMEM((WIDTH, HID), BF16),
            pltpu.VMEM((WIDTH, HID), BF16),
            pltpu.VMEM((HID, HID), BF16),
            pltpu.VMEM((HID, WIDTH), BF16),
            pltpu.VMEM((HID, WIDTH), BF16),
            pltpu.VMEM((HID, 128), BF16),
            pltpu.VMEM((HID, HID), BF16),
            pltpu.VMEM((CH, HID), BF16),
            pltpu.VMEM((8 * 128, 2 * ATOMS), BF16),
            pltpu.VMEM((8, GHOSTS, WIDTH), BF16),
            pltpu.VMEM((8, GHOSTS, WIDTH), BF16),
            pltpu.VMEM((64, 128), F32),
            pltpu.VMEM((4, SLOTS, ATOMS), F32),
            pltpu.VMEM((7, SLOTS, ATOMS), F32),
            pltpu.VMEM((ATOMS + 8 * GHOSTS, EDGES), BF16),
            pltpu.VMEM((128, EDGES), BF16),
            pltpu.VMEM((32, EDGES), BF16),
            pltpu.VMEM((SLOTS, HID, ATOMS), F32),
            pltpu.VMEM((SLOTS, HID, ATOMS), F32),
            pltpu.VMEM((WIDTH, EDGES), BF16),
            pltpu.VMEM((HID, 4 * ATOMS), BF16),
            pltpu.VMEM((HID, 4 * ATOMS), BF16),
            pltpu.VMEM((SLOTS // 2, CH, 4 * ATOMS), F32),
            pltpu.VMEM((8, 8, 128), F32),
            pltpu.VMEM((8, 8, 128), F32),
            pltpu.SemaphoreType.DMA((15,)),
            pltpu.SemaphoreType.DMA((8,)),
            pltpu.SemaphoreType.DMA((8,)),
            pltpu.SemaphoreType.DMA((8,)),
            pltpu.SemaphoreType.DMA((8,)),
        ],
        compiler_params=pltpu.CompilerParams(
            collective_id=0, has_side_effects=True, vmem_limit_bytes=56 * 1024 * 1024
        ),
        cost_estimate=pl.CostEstimate(
            flops=14_000_000_000, bytes_accessed=4_000_000, transcendentals=4_000_000
        ),
    )(
        features[0, 0],
        displacement.reshape(3, 1, EDGES),
        neighbours[0],
        neighbour_count[0],
        species[0],
        send_list[0, 0],
        send_count[0],
        w_center,
        w_neighbour,
        w_radial,
        w_hidden,
        w_tensor.T,
        readout[None],
        species_scale[None],
        species_shift[None],
    )
    energy, forces = pl.pallas_call(
        hand_over,
        out_shape=(
            jax.ShapeDtypeStruct((1, ATOMS), F32),
            jax.ShapeDtypeStruct((3, 1, ATOMS), F32),
        ),
        in_specs=[hbm],
        out_specs=(hbm, hbm),
        scratch_shapes=[pltpu.SemaphoreType.DMA((2,))],
    )(both)
    return energy[None], forces.reshape(1, 1, 3, ATOMS)


def solution(mesh):
    placed = (
        P("gx", "gy", None, None),
        P("gx", "gy", None, None),
        P("gx", "gy", None),
        P("gx", "gy", None),
        P("gx", "gy", None),
        P("gx", "gy", None, None),
        P("gx", "gy", None),
        P(),
        P(),
        P(),
        P(),
        P(),
        P(),
        P(),
        P(),
    )
    return jax.shard_map(
        shards,
        mesh=mesh,
        in_specs=placed,
        out_specs=(P("gx", "gy", None), P("gx", "gy", None, None)),
        check_vma=False,
    )
```

```python
import jax
import jax.numpy as jnp
from jax import lax
from jax.experimental import pallas as pl
from jax.experimental.pallas import tpu as pltpu
from jax.sharding import PartitionSpec as P

DIRECTIONS = ((-1, -1), (-1, 0), (-1, 1), (0, -1), (0, 1), (1, -1), (1, 0), (1, 1))
ATOMS = 256
SLOTS = 8
EDGES = ATOMS * SLOTS
GHOSTS = 192
WIDTH = 256
HID = 1024
CH = 64
F32 = jnp.float32
BF16 = jnp.bfloat16
MESH = pl.DeviceIdType.MESH


def iota(shape, dim):
    return lax.broadcasted_iota(jnp.int32, shape, dim)


def one_hot(hit):
    return jnp.where(hit, 1.0, 0.0).astype(BF16)


def dot(a, b):
    return jnp.dot(a, b, preferred_element_type=F32)


def silu_pair(value):
    gate = 0.5 * jnp.tanh(0.5 * value) + 0.5
    act = value * gate
    return act, gate + act * (1.0 - gate)


def split(value):
    high = value.astype(BF16)
    return high, (value - high.astype(F32)).astype(BF16)


def kernel(
    feat_hbm,
    disp_hbm,
    nbr_hbm,
    cnt_hbm,
    spc_hbm,
    lists_hbm,
    scnt_hbm,
    wc_hbm,
    wn_hbm,
    wr_hbm,
    wh_hbm,
    wtt_hbm,
    ro_hbm,
    sscale_hbm,
    sshift_hbm,
    out_ref,
    feat,
    disp,
    nbr,
    cnt,
    spc,
    lists,
    scnt,
    wr,
    ro,
    sscale,
    sshift,
    wc,
    wn,
    wh,
    wct,
    wnt,
    wrt,
    wht,
    wtt,
    sel,
    outg,
    ghost,
    stage,
    dsp,
    geo,
    oh,
    low_hot,
    high_hot,
    pre,
    drad,
    rows,
    act1,
    act2,
    tws,
    back_out,
    back_in,
    load_sem,
    send_sem,
    recv_sem,
    bsend_sem,
    brecv_sem,
):
    px, qy = lax.axis_index("gx"), lax.axis_index("gy")
    nx, ny = lax.axis_size("gx"), lax.axis_size("gy")

    def peer(ox, oy):
        return lax.rem(px + (ox + nx), nx), lax.rem(qy + (oy + ny), ny)

    core = lax.rem(qy, 2)
    side = 2 * core - 1
    order = [
        (4 - core, peer(0, -side), 0),
        (6 + side, peer(1, side), 1),
        (1 + side, peer(-1, side), 2),
        (3 + core, peer(0, side), 3),
        (6 - side, peer(1, -side), 4),
        (1 - side, peer(-1, -side), 5),
        (6, peer(1, 0), 6),
        (1, peer(-1, 0), 7),
    ]
    origin = [
        (4 - core, peer(0, -side)),
        (1 + side, peer(-1, side)),
        (6 + side, peer(1, side)),
        (3 + core, peer(0, side)),
        (1 - side, peer(-1, -side)),
        (6 - side, peer(1, -side)),
        (1, peer(-1, 0)),
        (6, peer(1, 0)),
    ]
    base = [(ATOMS + GHOSTS * block + jnp.int32(0)).astype(F32) for block, _ in origin]
    barrier = pltpu.get_barrier_semaphore()
    for _, device, _ in order[1:] + order[:1]:
        pl.semaphore_signal(barrier, inc=1, device_id=device, device_id_type=MESH)

    pairs = (
        (lists_hbm, lists),
        (scnt_hbm, scnt),
        (feat_hbm, feat),
        (disp_hbm, disp),
        (nbr_hbm, nbr),
        (cnt_hbm, cnt),
        (spc_hbm, spc),
        (sscale_hbm, sscale),
        (sshift_hbm, sshift),
        (ro_hbm, ro),
        (wr_hbm, wr),
        (wc_hbm, wc),
        (wn_hbm, wn),
        (wh_hbm, wh),
        (wtt_hbm, wtt),
    )
    loads = [
        pltpu.make_async_copy(src, dst, load_sem.at[num]) for num, (src, dst) in enumerate(pairs)
    ]
    for load in loads:
        load.start()
    for load in loads[0:3]:
        load.wait()

    ids = jnp.concatenate([lists[...].astype(F32), jnp.zeros((8, ATOMS - GHOSTS), F32)], axis=1)
    slot = iota((ATOMS, 8), 0)
    kept = jnp.where((slot < scnt[...]) & (slot < GHOSTS), jnp.transpose(ids), -1.0)
    lane = iota((ATOMS, ATOMS), 1).astype(F32)
    for num in range(8):
        hit = one_hot(kept[:, num : num + 1] == lane)
        for half in range(2):
            sel[num * 128 : (num + 1) * 128, half * 256 : (half + 1) * 256] = hit[
                half * 128 : (half + 1) * 128
            ]
        outg[num] = dot(hit[0:GHOSTS], feat[...]).astype(BF16)
    pl.semaphore_wait(barrier, 8)
    sends = []
    for num, device, place in order:
        copy = pltpu.make_async_remote_copy(
            src_ref=outg.at[num],
            dst_ref=ghost.at[place],
            send_sem=send_sem.at[place],
            recv_sem=recv_sem.at[place],
            device_id=device,
            device_id_type=MESH,
        )
        copy.start()
        sends.append(copy)

    for load in loads[3:11]:
        load.wait()

    for axis in range(3):
        for c in range(16):
            stage[pl.ds(axis * 16 + c, 1), :] = disp[axis, :, c * 128 : (c + 1) * 128]
    for c in range(16):
        stage[pl.ds(48 + c, 1), :] = nbr[0:1, c * 128 : (c + 1) * 128].astype(F32)
    turned = jnp.transpose(stage[...])
    for row in range(4):
        for a in range(16):
            dsp[row, :, a * 16 : (a + 1) * 16] = turned[
                a * 8 : (a + 1) * 8, row * 16 : (row + 1) * 16
            ]
    col = iota((ATOMS, ATOMS), 1)
    swap = iota((ATOMS, ATOMS), 0) == (col & 15) * 16 + (col >> 4)
    swap_b = one_hot(swap)
    small = jnp.concatenate(
        [cnt[...].astype(F32), spc[...].astype(F32), jnp.zeros((14, ATOMS), F32)], axis=0
    ).astype(BF16)
    small = dot(small, swap_b)
    count, kind = small[0:1], small[1:2]
    scale = jnp.zeros((1, ATOMS), F32)
    shift = jnp.zeros((1, ATOMS), F32)
    for num in range(4):
        hit = kind == float(num)
        scale = jnp.where(hit, sscale[0:1, num : num + 1], scale)
        shift = jnp.where(hit, sshift[0:1, num : num + 1], shift)
    squared = dsp[0] * dsp[0] + dsp[1] * dsp[1] + dsp[2] * dsp[2]
    distance = jnp.sqrt(squared)
    inverse = 1.0 / distance
    live = jnp.where(iota((SLOTS, ATOMS), 0).astype(F32) < count, 1.0, 0.0)
    for axis in range(3):
        geo[axis] = dsp[axis] * inverse
    geo[3] = jnp.square(1.0 - squared) * live
    geo[4] = distance
    geo[5] = -4.0 * (1.0 - squared) * live
    geo[6] = inverse

    wrt[...] = jnp.transpose(
        jnp.concatenate([wr[...].astype(F32), jnp.zeros((120, HID), F32)], axis=0)
    ).astype(BF16)
    loads[11].wait()
    for num in range(4):
        wct[num * 256 : (num + 1) * 256, :] = jnp.transpose(wc[:, num * 256 : (num + 1) * 256])
    loads[12].wait()
    for num in range(4):
        wnt[num * 256 : (num + 1) * 256, :] = jnp.transpose(wn[:, num * 256 : (num + 1) * 256])
    loads[13].wait()

    def turn(num, carry):
        start = pl.multiple_of(num * 256, 256)
        for part in range(4):
            wht[pl.ds(start, 256), part * 256 : (part + 1) * 256] = jnp.transpose(
                wh[part * 256 : (part + 1) * 256, pl.ds(start, 256)]
            )
        return carry

    lax.fori_loop(0, 4, turn, 0)
    loads[14].wait()

    feat_t = jnp.transpose(feat[...])
    feat_p = dot(feat_t, swap_b).astype(BF16)
    unit_id = iota((16, ATOMS), 0)
    centre_at = (unit_id.astype(F32) + 1.0) * 0.125
    row_id = iota((256, ATOMS), 0).astype(F32)

    def before(k, carry):
        lanes = pl.ds(pl.multiple_of(k * 256, 256), 256)
        ids = dsp[3, pl.ds(k, 1), :]
        oh[0:ATOMS, lanes] = one_hot(row_id == ids)
        inside = ids
        place = jnp.full((1, ATOMS), 16.0, F32)
        for num in range(8):
            start = ATOMS + num * GHOSTS
            away = ids - base[num]
            oh[start : start + GHOSTS, lanes] = one_hot(row_id[0:GHOSTS] == away)
            hit = (away >= 0.0) & (away < float(GHOSTS))
            inside = jnp.where(hit, away, inside)
            place = jnp.where(hit, 2.0 * num, place)
        rows[:, lanes] = dot(feat_t, oh[0:256, lanes]).astype(BF16)
        upper = jnp.where(inside >= 128.0, 1.0, 0.0)
        low_hot[:, lanes] = one_hot(row_id[0:128] == inside - 128.0 * upper)
        high_hot[:, lanes] = one_hot(row_id[0:32] == place + upper)
        offset = (geo[4, pl.ds(k, 1), :] - centre_at) * 4.0
        basis = jnp.where(unit_id < 8, jnp.exp(-offset * offset), 0.0)
        both = jnp.concatenate([basis, -8.0 * offset * basis], axis=1).astype(BF16)
        both = jnp.concatenate([both, jnp.zeros((112, 512), BF16)], axis=0)
        for part in range(4):
            here = slice(part * 256, (part + 1) * 256)
            radial = dot(wrt[here, :], both)
            pre[k, here, :] = radial[:, :256] + dot(wct[here, :], feat_p)
            drad[k, here, :] = radial[:, 256:]
        return carry

    lax.fori_loop(0, SLOTS, before, 0)

    def landed_rows(start, stop):
        for num in range(start, stop):
            sends[num].wait_recv()
        return jnp.transpose(
            jnp.concatenate([ghost[num] for num in range(start, stop)], axis=0)
        )

    for start, stop in ((0, 1), (1, 4), (4, 8)):
        turned = landed_rows(start, stop)
        ids = slice(ATOMS + start * GHOSTS, ATOMS + stop * GHOSTS)
        for part in range(4):
            here = slice(part * 512, (part + 1) * 512)
            rows[:, here] = rows[:, here] + dot(turned, oh[ids, here]).astype(BF16)

    def first(k, at):
        lanes = slice(k * 256, (k + 1) * 256)
        found = rows[:, lanes]
        summed = dot(wnt[...], found)
        for part in range(4):
            here = slice(part * 256, (part + 1) * 256)
            act, slope = silu_pair(summed[here] + pre[k, here, :])
            act1[here, at : at + 256] = act.astype(BF16)
            act1[here, at + 256 : at + 512] = (slope * drad[k, here, :]).astype(BF16)

    def second(at):
        for part in range(4):
            here = slice(part * 256, (part + 1) * 256)
            hidden = dot(wht[here, :], act1[:, at : at + 512])
            act, slope = silu_pair(hidden[:, :256])
            act2[here, at : at + 256] = act.astype(BF16)
            act2[here, at + 256 : at + 512] = (slope * hidden[:, 256:]).astype(BF16)

    def product(k, weight, sums):
        unit = [geo[axis, k : k + 1, :] for axis in range(3)]
        row = rows[:, k * 256 : (k + 1) * 256].astype(F32)
        s, v = row[0:CH], [row[CH * (m + 1) : CH * (m + 2)] for m in range(3)]
        w = weight[:, :256] * geo[3, k : k + 1, :]
        out = [sums[0] + w * (s + unit[0] * v[0] + unit[1] * v[1] + unit[2] * v[2])]
        for m in range(3):
            out.append(sums[m + 1] + w * (s * unit[m] + v[m]))
        return tuple(out)

    sums = tuple(jnp.zeros((CH, ATOMS), F32) for _ in range(4))
    for k in range(0, SLOTS, 2):
        first(k, 0)
        first(k + 1, 512)
        second(0)
        second(512)
        tws[k // 2] = dot(wtt[...], act2[...])
    for k in range(SLOTS):
        sums = product(k, tws[k // 2, :, (k % 2) * 512 : (k % 2) * 512 + 512], sums)

    eye = iota((CH, CH), 0) == iota((CH, CH), 1)
    read = jnp.sum(jnp.where(eye, ro[...], 0.0), axis=1, keepdims=True)
    inv = sums[0] * sums[0] + sums[1] * sums[1] + sums[2] * sums[2] + sums[3] * sums[3]
    energy = scale * jnp.sum(inv * read, axis=0, keepdims=True) + shift
    factor = 2.0 * scale * read
    cot = [factor * total for total in sums]

    def slopes(k, own, landed):
        lanes = slice(k * 256, (k + 1) * 256)
        unit = [geo[axis, pl.ds(k, 1), :] for axis in range(3)]
        env = geo[3, pl.ds(k, 1), :]
        row = rows[:, lanes].astype(F32)
        s, v = row[0:CH], [row[CH * (m + 1) : CH * (m + 2)] for m in range(3)]
        weight = tws[k // 2, :, (k % 2) * 512 : (k % 2) * 512 + 512]
        tw, dtw = weight[:, :256], weight[:, 256:]
        q = cot[0] * (s + unit[0] * v[0] + unit[1] * v[1] + unit[2] * v[2])
        for m in range(3):
            q = q + cot[m + 1] * (s * unit[m] + v[m])
        by_dist = env * jnp.sum(q * dtw, axis=0, keepdims=True)
        by_env = jnp.sum(q * tw, axis=0, keepdims=True)
        w = tw * env
        by_unit = [
            jnp.sum(w * (cot[0] * v[m] + cot[m + 1] * s), axis=0, keepdims=True) for m in range(3)
        ]
        along = by_unit[0] * unit[0] + by_unit[1] * unit[1] + by_unit[2] * unit[2]
        inverse_k = geo[6, pl.ds(k, 1), :]
        common = by_dist - along * inverse_k
        scaled = by_env * geo[5, pl.ds(k, 1), :]
        grad = jnp.concatenate(
            [
                common * unit[m] + scaled * dsp[m, pl.ds(k, 1), :] + by_unit[m] * inverse_k
                for m in range(3)
            ]
            + [jnp.zeros((5, ATOMS), F32)],
            axis=0,
        )
        high, low = split(grad[0:3])
        flat = jnp.concatenate([high, low], axis=0)
        spread = lax.dot_general(
            jnp.concatenate([high_hot[:, lanes] * flat[m : m + 1] for m in range(6)], axis=0),
            low_hot[:, lanes],
            (((1,), (1,)), ((), ())),
            preferred_element_type=F32,
        )
        return own + grad, landed + spread

    own = jnp.zeros((8, ATOMS), F32)
    landed = jnp.zeros((192, 128), F32)
    for k in range(SLOTS):
        own, landed = slopes(k, own, landed)
    landed = landed[0:96] + landed[96:192]
    for num in range(8):
        pair = [landed[m * 32 + 2 * num : m * 32 + 2 * num + 2] for m in range(3)]
        none = jnp.zeros((1, 128), F32)
        back_out[num] = jnp.concatenate(
            [side_row for half in range(2) for side_row in [p[half : half + 1] for p in pair] + [none]],
            axis=0,
        )
    returns = []
    for place in (1, 2, 3, 4, 5, 6, 7, 0):
        block, device = origin[place]
        copy = pltpu.make_async_remote_copy(
            src_ref=back_out.at[place],
            dst_ref=back_in.at[7 - block],
            send_sem=bsend_sem.at[place],
            recv_sem=brecv_sem.at[7 - block],
            device_id=device,
            device_id_type=MESH,
        )
        copy.start()
        returns.append(copy)
    tail = jnp.concatenate([own[0:3], energy, jnp.zeros((4, ATOMS), F32)], axis=0)
    tail = jnp.dot(
        tail, jnp.where(swap, 1.0, 0.0), preferred_element_type=F32, precision=lax.Precision.HIGHEST
    )
    total = tail[0:3] - jnp.concatenate(
        [
            jnp.concatenate([landed[m * 32 + 16 + half : m * 32 + 17 + half] for m in range(3)], axis=0)
            for half in range(2)
        ],
        axis=1,
    )
    for copy in returns:
        copy.wait_recv()
    back = jnp.concatenate([back_in[num] for num in range(8)], axis=1)
    both = dot(jnp.concatenate(split(back), axis=0), sel[...])
    both = both[0:8] + both[8:16]
    total = total + both[0:3, 0:ATOMS] + both[4:7, ATOMS:]
    for copy in sends + returns:
        copy.wait_send()
    for axis in range(3):
        out_ref[axis] = total[axis : axis + 1]
    out_ref[3] = tail[3:4]


def hand_over(both, en_ref, fo_ref, sem):
    energy = pltpu.make_async_copy(both.at[3], en_ref, sem.at[0])
    forces = pltpu.make_async_copy(both.at[pl.ds(0, 3)], fo_ref, sem.at[1])
    energy.start()
    forces.start()
    energy.wait()
    forces.wait()


def shards(
    features,
    displacement,
    neighbours,
    neighbour_count,
    species,
    send_list,
    send_count,
    w_center,
    w_neighbour,
    w_radial,
    w_hidden,
    w_tensor,
    readout,
    species_scale,
    species_shift,
):
    vmem = pl.BlockSpec(memory_space=pltpu.VMEM)
    hbm = pl.BlockSpec(memory_space=pl.ANY)
    both = pl.pallas_call(
        kernel,
        out_shape=jax.ShapeDtypeStruct((4, 1, ATOMS), F32),
        in_specs=[hbm] * 15,
        out_specs=vmem,
        scratch_shapes=[
            pltpu.VMEM((ATOMS, WIDTH), BF16),
            pltpu.VMEM((3, 1, EDGES), F32),
            pltpu.VMEM((1, EDGES), jnp.int32),
            pltpu.VMEM((1, ATOMS), jnp.int32),
            pltpu.VMEM((1, ATOMS), jnp.int32),
            pltpu.VMEM((8, GHOSTS), jnp.int32),
            pltpu.VMEM((1, 8), jnp.int32),
            pltpu.VMEM((8, HID), BF16),
            pltpu.VMEM((1, CH), F32),
            pltpu.VMEM((1, 4), F32),
            pltpu.VMEM((1, 4), F32),
            pltpu.VMEM((WIDTH, HID), BF16),
            pltpu.VMEM((WIDTH, HID), BF16),
            pltpu.VMEM((HID, HID), BF16),
            pltpu.VMEM((HID, WIDTH), BF16),
            pltpu.VMEM((HID, WIDTH), BF16),
            pltpu.VMEM((HID, 128), BF16),
            pltpu.VMEM((HID, HID), BF16),
            pltpu.VMEM((CH, HID), BF16),
            pltpu.VMEM((8 * 128, 2 * ATOMS), BF16),
            pltpu.VMEM((8, GHOSTS, WIDTH), BF16),
            pltpu.VMEM((8, GHOSTS, WIDTH), BF16),
            pltpu.VMEM((64, 128), F32),
            pltpu.VMEM((4, SLOTS, ATOMS), F32),
            pltpu.VMEM((7, SLOTS, ATOMS), F32),
            pltpu.VMEM((ATOMS + 8 * GHOSTS, EDGES), BF16),
            pltpu.VMEM((128, EDGES), BF16),
            pltpu.VMEM((32, EDGES), BF16),
            pltpu.VMEM((SLOTS, HID, ATOMS), F32),
            pltpu.VMEM((SLOTS, HID, ATOMS), F32),
            pltpu.VMEM((WIDTH, EDGES), BF16),
            pltpu.VMEM((HID, 4 * ATOMS), BF16),
            pltpu.VMEM((HID, 4 * ATOMS), BF16),
            pltpu.VMEM((SLOTS // 2, CH, 4 * ATOMS), F32),
            pltpu.VMEM((8, 8, 128), F32),
            pltpu.VMEM((8, 8, 128), F32),
            pltpu.SemaphoreType.DMA((15,)),
            pltpu.SemaphoreType.DMA((8,)),
            pltpu.SemaphoreType.DMA((8,)),
            pltpu.SemaphoreType.DMA((8,)),
            pltpu.SemaphoreType.DMA((8,)),
        ],
        compiler_params=pltpu.CompilerParams(
            collective_id=0, has_side_effects=True, vmem_limit_bytes=56 * 1024 * 1024
        ),
        cost_estimate=pl.CostEstimate(
            flops=14_000_000_000, bytes_accessed=4_000_000, transcendentals=4_000_000
        ),
    )(
        features[0, 0],
        displacement.reshape(3, 1, EDGES),
        neighbours[0],
        neighbour_count[0],
        species[0],
        send_list[0, 0],
        send_count[0],
        w_center,
        w_neighbour,
        w_radial,
        w_hidden,
        w_tensor.T,
        readout[None],
        species_scale[None],
        species_shift[None],
    )
    energy, forces = pl.pallas_call(
        hand_over,
        out_shape=(
            jax.ShapeDtypeStruct((1, ATOMS), F32),
            jax.ShapeDtypeStruct((3, 1, ATOMS), F32),
        ),
        in_specs=[hbm],
        out_specs=(hbm, hbm),
        scratch_shapes=[pltpu.SemaphoreType.DMA((2,))],
    )(both)
    return energy[None], forces.reshape(1, 1, 3, ATOMS)


def solution(mesh):
    placed = (
        P("gx", "gy", None, None),
        P("gx", "gy", None, None),
        P("gx", "gy", None),
        P("gx", "gy", None),
        P("gx", "gy", None),
        P("gx", "gy", None, None),
        P("gx", "gy", None),
        P(),
        P(),
        P(),
        P(),
        P(),
        P(),
        P(),
        P(),
    )
    return jax.shard_map(
        shards,
        mesh=mesh,
        in_specs=placed,
        out_specs=(P("gx", "gy", None), P("gx", "gy", None, None)),
        check_vma=False,
    )
```
